768 devices in a mesh: axial: 192 (over z, y, core), azim: 4 (over x).
Axes of the slice: x: 4, y: 8, z: 12, core: 2. Of those that a mesh axis runs over, the one named last changes fastest.
Arguments:
- tet_state: bfloat16 [175, 786432], P(None, ('axial', 'azim')), may hold values from -6 to 6
- prism_state: bfloat16 [375, 786432], P(None, ('axial', 'azim')), may hold values from -6 to 6
- tet_volume: bfloat16 [175, 175], replicated, may hold values from -0.4375 to 0.4375
- prism_volume: bfloat16 [375, 375], replicated, may hold values from -0.3125 to 0.3125
- face_extrap: bfloat16 [300, 175], replicated, may hold values from -0.4375 to 0.4375
- face_lift: bfloat16 [175, 300], replicated, may hold values from -0.75 to 0.75
- wall_extrap: bfloat16 [75, 375], replicated, may hold values from -0.3125 to 0.3125
- wall_lift: bfloat16 [375, 75], replicated, may hold values from -0.75 to 0.75
- face_code: int32 [786432], P(('axial', 'azim')), may hold values from 0 to 4095, as said below
- face_count: int32 [768, 2], P(('axial', 'azim')), may hold values from 0 to 512, as said below
- face_area: float32 [786432], P(('axial', 'azim')), may hold values from 0.5 to 2
- burn_prism: int32 [393216], P(('axial', 'azim')), may hold values from 0 to 1023, as said below
- burn_owner: int32 [393216, 1], P(('axial', 'azim')), may hold values from 0 to 3; in each aligned block of 512 rows (0 to 511, 512 to 1023, ...) at most 128 rows name the same one
- burn_law: float32 [192, 4, 6], P('axial'), may hold values from 0.5 to 2
Outputs:
- tet_new: bfloat16 [175, 786432], P(None, ('axial', 'azim'))
- prism_new: bfloat16 [375, 786432], P(None, ('axial', 'azim'))
The draws below stay inside these ranges and needn't reach their ends.
Inputs may be any that keep to these rules, and one draw needn't show every extreme that they name: `face_code`: within each partition's block of 1024 entries the codes are distinct; the first 512 are faces shared with the lower axial neighbour, the rest with the upper; upper slot s of (a, z) is the same face as lower slot s of (a+1, z). `face_count`: column 0 counts live lower slots, column 1 live upper slots; the upper count of (a, z) equals the lower count of (a+1, z); zero at the two ends of the axial range, 1 or more elsewhere; 512 is reached. `burn_prism`: distinct within each partition's block. `burn_owner`: at most 128 wall faces of one partition name one owner, and that bound is reached.
All inputs are finite; a program needn't handle non-finite values.
Results may differ from the reference program's by a relative error of at most 0.0043.
Values may be sent and summed in bfloat16 or wider, within the bound.
No kernel may reach another device: no remote copies, remote signals or barrier semaphores. Data moves between devices by JAX's collectives and lax.ppermute only.
A program may use at most 32 MiB of HBM per device.

```python
import math
import jax
import jax.numpy as jnp
import numpy as np
from jax import lax

NV = 5
TFP = 15
TW = 175
PW = 375
FW = 75
ET = 1024
EP = 1024
CF = 512
BW_DEV = 512
CB = 128
SLABS = 192
SECTORS = 4
TETS = 786432
PRISMS = 786432


def draw_face_code(key, part):
    subkeys = jax.random.split(key, SLABS * SECTORS)

    def per_device(subkey):
        return jax.random.permutation(subkey, 4 * ET)[:2 * CF].astype(jnp.int32)
    return jax.vmap(per_device)(subkeys).reshape(SLABS * SECTORS * 2 * CF).astype(jnp.int32)


def draw_face_count(key, part):
    key_count, key_pick = jax.random.split(key)
    pairs = jax.random.randint(key_count, (SLABS - 1, SECTORS), 1, CF + 1).astype(jnp.int32)
    flat_pairs = pairs.reshape((SLABS - 1) * SECTORS)
    picked = jax.random.randint(key_pick, (), 0, (SLABS - 1) * SECTORS).astype(jnp.int32)
    flat_pairs = jnp.where(jnp.arange((SLABS - 1) * SECTORS, dtype=jnp.int32) == picked, CF, flat_pairs)
    pairs = flat_pairs.reshape(SLABS - 1, SECTORS)
    zeros_row = jnp.zeros((1, SECTORS), jnp.int32)
    lower = jnp.concatenate([zeros_row, pairs], axis=0)
    upper = jnp.concatenate([pairs, zeros_row], axis=0)
    return jnp.stack([lower, upper], axis=-1).reshape(SLABS * SECTORS, 2).astype(jnp.int32)


def draw_burn_prism(key, part):
    subkeys = jax.random.split(key, SLABS * SECTORS)

    def per_device(subkey):
        return jax.random.permutation(subkey, EP)[:BW_DEV].astype(jnp.int32)
    return jax.vmap(per_device)(subkeys).reshape(SLABS * SECTORS * BW_DEV).astype(jnp.int32)


def block_scale(key, extent, cuts, smallest, high):
    factor_of, own = 1.0, jax.random.fold_in(key, 6)
    for position, parts in cuts:
        steps = jnp.exp(jax.random.uniform(jax.random.fold_in(own, position), (parts,), jnp.float32, smallest / len(cuts), high / len(cuts)))
        factor_of = factor_of * jnp.repeat(steps, extent[position] // parts).reshape([-1 if axis == position else 1 for axis in range(len(extent))])
    return factor_of


def routed_block(stream_key, own, number, rows, number_of, top, reach, slope):
    order = jax.random.permutation(stream_key, number_of)
    heavy_load, common = shares(number_of, rows * top, reach, slope, True), shares(number_of, rows * top, reach, slope, False)
    places = jnp.arange(number_of)

    def named(sizes, turn):
        used = int((sizes > 0).sum())
        fixed = max(1, used // 4)
        passed = fixed + (places - fixed + turn * (used - fixed)) % max(1, number_of - fixed)
        return jnp.zeros((number_of,), jnp.int32).at[order[jnp.where(places < fixed, places, passed)]].set(jnp.asarray(sizes, jnp.int32))

    sizes = jnp.where(number % 4 == 0, named(heavy_load, number // 4), named(common, number - number // 4 - 1))
    mixed = jax.random.permutation(jax.random.fold_in(own, 3), number_of)
    giver, sink = mixed[0:number_of // 2 * 2:2], mixed[1:number_of // 2 * 2:2]
    slack = jnp.minimum(sizes[giver] - 1, reach - sizes[sink]) // 2
    slack = jnp.where((giver == order[0]) | (sink == order[0]) | (sizes[sink] == 0), 0, jnp.maximum(slack, 0))
    passed = jax.random.randint(jax.random.fold_in(own, 4), (number_of // 2,), 0, 1 << 20) % (slack + 1)
    sizes = sizes.at[giver].add(-passed).at[sink].add(passed)
    items = jnp.searchsorted(jnp.cumsum(sizes), jnp.arange(rows * top), side="right").astype(jnp.int32)
    grid = items.reshape(top, rows).T
    grid = grid[jax.random.permutation(jax.random.fold_in(own, 1), rows)]
    turn = jax.random.randint(jax.random.fold_in(own, 2), (rows, 1), 0, top)
    return jnp.take_along_axis(grid, (jnp.arange(top)[None, :] + turn) % top, axis=1)


def shares(count, total, reach, skew, full):
    portions = [(1 << 20) // math.isqrt(grade ** skew) + 1 for grade in range(1, count + 1)]
    largest = reach if full else min(reach, max(-(-total // count), total * portions[0] // sum(portions)))
    least = 1 if total - largest >= count - 1 else 0
    holding, rest = [largest] + [least] * (count - 1), total - largest - least * (count - 1)
    while rest > 0:
        candidates = [i for i in range(1, count) if holding[i] < largest] or [i for i in range(1, count) if holding[i] < reach]
        mass, budget = sum([portions[i] for i in candidates]), rest
        for i in candidates:
            addition = min(reach - holding[i], max(1, budget * portions[i] // mass), rest)
            holding[i] = holding[i] + addition
            rest = rest - addition
    return np.array(holding)


def normal_values(own_key, extent, spread, bound, pieces=(), kind=jnp.bfloat16):
    array = spread * jax.random.normal(own_key, extent, jnp.float32)
    if pieces:
        array = array * block_scale(own_key, extent, pieces, -0.22, 0.18)
    return jnp.clip(array, -bound, bound).astype(kind)


def setup_inputs(seed: int = 0) -> dict:
    keys = jax.random.split(jax.random.key(seed), 15)
    tet_state = normal_values(keys[0], (TW, TETS), 1.0, 6.0, ((1, 768),))
    prism_state = normal_values(keys[1], (PW, PRISMS), 1.0, 6.0, ((1, 768),))
    tet_volume = normal_values(keys[2], (TW, TW), TW ** -0.5, 0.4375)
    prism_volume = normal_values(keys[3], (PW, PW), PW ** -0.5, 0.3125)
    face_extrap = normal_values(keys[4], (4 * FW, TW), TW ** -0.5, 0.4375)
    face_lift = normal_values(keys[5], (TW, 4 * FW), FW ** -0.5, 0.75)
    wall_extrap = normal_values(keys[6], (FW, PW), PW ** -0.5, 0.3125)
    wall_lift = normal_values(keys[7], (PW, FW), FW ** -0.5, 0.75)
    face_code = draw_face_code(jax.random.fold_in(keys[14], 71), 0)
    face_count = draw_face_count(jax.random.fold_in(keys[14], 71), 0)
    face_area = jnp.clip(jnp.exp(math.log(2.0) - 1.3862944 * jax.random.uniform(keys[10], (SLABS * SECTORS * 2 * CF,), jnp.float32) ** block_scale(keys[10], (SLABS * SECTORS * 2 * CF,), ((0, 768),), -0.2, 0.2)), 0.5, 2.0)
    burn_prism = draw_burn_prism(jax.random.fold_in(keys[14], 71), 0)
    burn_owner_keys = jax.random.split(jax.random.fold_in(keys[12], 1), (SLABS * SECTORS * BW_DEV) // BW_DEV)
    burn_owner_turns = jax.random.permutation(jax.random.fold_in(keys[12], 3), (SLABS * SECTORS * BW_DEV) // BW_DEV)
    burn_owner = jax.vmap(lambda own, number: routed_block(jax.random.fold_in(keys[12], 2), own, number, BW_DEV, SECTORS, 1, CB, 2))(burn_owner_keys, burn_owner_turns).reshape((SLABS * SECTORS * BW_DEV, 1))
    burn_law = jnp.clip(0.5 + 1.5 * jax.random.uniform(keys[13], (SLABS, SECTORS, 6), jnp.float32) ** block_scale(keys[13], (SLABS, SECTORS, 6), ((0, 192),), -0.2, 0.2), 0.5, 2.0)
    return {"tet_state": tet_state, "prism_state": prism_state, "tet_volume": tet_volume, "prism_volume": prism_volume, "face_extrap": face_extrap, "face_lift": face_lift, "wall_extrap": wall_extrap, "wall_lift": wall_lift, "face_code": face_code, "face_count": face_count, "face_area": face_area, "burn_prism": burn_prism, "burn_owner": burn_owner, "burn_law": burn_law}


section_step = 0.25


def square_half(values):
    widened = values.astype(jnp.float32)
    return (0.5 * widened * widened).astype(jnp.bfloat16)


def product(left, right):
    return jnp.dot(left.astype(jnp.float32), right.astype(jnp.float32), precision=lax.Precision.HIGHEST, preferred_element_type=jnp.float32)


def reference(tet_state, prism_state, tet_volume, prism_volume, face_extrap, face_lift, wall_extrap, wall_lift, face_code, face_count, face_area, burn_prism, burn_owner, burn_law):
    partitions = SLABS * SECTORS
    slots = 2 * CF
    face_ids = jnp.arange(4, dtype=jnp.int32)

    def left_of(device):
        tet_block = lax.dynamic_slice_in_dim(tet_state, device * ET, ET, 1)
        codes = lax.dynamic_slice_in_dim(face_code, device * slots, slots, 0)
        columns = jnp.take(tet_block, codes // 4, axis=1)
        extended = product(face_extrap, columns).reshape(4, FW, slots)
        chosen = (codes % 4)[None, :] == face_ids[:, None]
        return jnp.sum(jnp.where(chosen[:, None, :], extended, jnp.zeros_like(extended)), axis=0).astype(jnp.bfloat16)

    left_all = lax.map(left_of, jnp.arange(partitions, dtype=jnp.int32))
    face_grid = left_all.reshape(SLABS, SECTORS, FW, 2, CF)
    zeros_row = jnp.zeros((1, SECTORS, FW, CF), jnp.bfloat16)
    from_lower = jnp.concatenate([zeros_row, face_grid[:-1, :, :, 1]], axis=0)
    from_upper = jnp.concatenate([face_grid[1:, :, :, 0], zeros_row], axis=0)
    right_all = jnp.stack([from_lower, from_upper], axis=3).reshape(partitions, FW, slots)

    def wall_of(device):
        prism_block = lax.dynamic_slice_in_dim(prism_state, device * EP, EP, 1)
        prism_index = lax.dynamic_slice_in_dim(burn_prism, device * BW_DEV, BW_DEV, 0)
        columns = jnp.take(prism_block, prism_index, axis=1)
        return product(wall_extrap, columns).astype(jnp.bfloat16)

    wall_all = lax.map(wall_of, jnp.arange(partitions, dtype=jnp.int32))
    pressure = wall_all[:, 4 * TFP:5 * TFP, :].astype(jnp.float32)
    squares = pressure * pressure
    row_sums = jnp.sum(squares, axis=1)
    owners = burn_owner.reshape(partitions, BW_DEV)
    owner_hot = (owners[:, :, None] == jnp.arange(SECTORS, dtype=jnp.int32)[None, None, :]).astype(jnp.float32)
    patch_parts = jnp.einsum("pb,pbs->ps", row_sums, owner_hot, precision=lax.Precision.HIGHEST)
    totals = jnp.sum(patch_parts.reshape(SLABS, SECTORS, SECTORS), axis=1)
    burn_coef = burn_law[:, :, 0]
    damping = 1.0 / (1.0 + burn_coef * totals / (BW_DEV * TFP))
    law_rows = jnp.repeat(burn_law, SECTORS, axis=0)
    damp_rows = jnp.repeat(damping, SECTORS, axis=0)
    coef_each = jnp.sum(owner_hot * law_rows[:, None, :, 0], axis=2)
    damp_each = jnp.sum(owner_hot * damp_rows[:, None, :], axis=2)
    inject_each = jnp.einsum("pbs,psv->pvb", owner_hot, law_rows[:, :, 1:6], precision=lax.Precision.HIGHEST)
    wall_jump = (inject_each[:, :, None, :] * (coef_each * damp_each)[:, None, None, :] * squares[:, None, :, :]
                 - wall_all.reshape(partitions, NV, TFP, BW_DEV).astype(jnp.float32)).astype(jnp.bfloat16)
    wall_jump = wall_jump.reshape(partitions, FW, BW_DEV)

    normal = jnp.concatenate([-jnp.ones((CF,), jnp.float32), jnp.ones((CF,), jnp.float32)])
    slot_index = jnp.arange(CF, dtype=jnp.int32)

    def finish(device):
        tet_block = lax.dynamic_slice_in_dim(tet_state, device * ET, ET, 1)
        tet_div = product(tet_volume, square_half(tet_block))
        codes = lax.dynamic_slice_in_dim(face_code, device * slots, slots, 0)
        counts = face_count[device]
        active = (slot_index[None, :] < counts[:, None]).reshape(slots)
        areas = lax.dynamic_slice_in_dim(face_area, device * slots, slots, 0)
        left_rows = left_all[device].astype(jnp.float32)
        right_rows = right_all[device].astype(jnp.float32)
        speed = jnp.maximum(jnp.abs(left_rows), jnp.abs(right_rows))
        flux_jump = 0.25 * normal * (right_rows * right_rows - left_rows * left_rows) - 0.5 * speed * (right_rows - left_rows)
        jump_rows = (jnp.where(active, areas, jnp.zeros_like(areas)) * flux_jump).astype(jnp.bfloat16)
        chosen = (codes % 4)[None, :] == face_ids[:, None]
        placed = jnp.where(chosen[:, None, :], jump_rows[None, :, :], jnp.zeros((4, FW, slots), jnp.bfloat16)).reshape(4 * FW, slots)
        tet_lift = product(face_lift, placed)
        tet_total = tet_div.at[:, codes // 4].add(tet_lift)
        tet_out = (tet_block.astype(jnp.float32) - section_step * tet_total).astype(jnp.bfloat16)
        prism_block = lax.dynamic_slice_in_dim(prism_state, device * EP, EP, 1)
        prism_div = product(prism_volume, square_half(prism_block))
        prism_index = lax.dynamic_slice_in_dim(burn_prism, device * BW_DEV, BW_DEV, 0)
        prism_lift = product(wall_lift, wall_jump[device])
        prism_total = prism_div.at[:, prism_index].add(prism_lift)
        prism_out = (prism_block.astype(jnp.float32) - section_step * prism_total).astype(jnp.bfloat16)
        return tet_out, prism_out

    tet_parts, prism_parts = lax.map(finish, jnp.arange(partitions, dtype=jnp.int32))
    tet_new = jnp.moveaxis(tet_parts, 0, 1).reshape(TW, TETS)
    prism_new = jnp.moveaxis(prism_parts, 0, 1).reshape(PW, PRISMS)
    return (tet_new, prism_new)
```

```python
import jax
import jax.numpy as jnp
from jax import lax
from jax.experimental import pallas as pl
from jax.experimental.pallas import tpu as pltpu
from jax.sharding import PartitionSpec as P

NV = 5
TFP = 15
FW = 75
FP = 80
BW_DEV = 512
SECTORS = 4
STEP = 0.25

BF = jnp.bfloat16
F32 = jnp.float32
NN = (((1,), (0,)), ((), ()))
NT = (((1,), (1,)), ((), ()))
TN = (((0,), (0,)), ((), ()))


def mm(a, b, dims=NN):
    return lax.dot_general(a, b, dims, preferred_element_type=F32)


def rows_of(shape):
    return lax.broadcasted_iota(jnp.int32, shape, 0)


def cols_of(shape):
    return lax.broadcasted_iota(jnp.int32, shape, 1)


def hot(mask):
    return jnp.where(mask, 1.0, 0.0).astype(BF)


def spread(rows, cols):
    r = rows_of((rows, cols))
    f = (r >= FP).astype(jnp.int32) + (r >= 2 * FP).astype(jnp.int32) + (r >= 3 * FP).astype(jnp.int32)
    c = cols_of((rows, cols))
    return hot((c == r - (FP - FW) * f) & (r - FP * f < FW))


def square_half(values):
    wide = values.astype(F32)
    return (0.5 * wide * wide).astype(BF)


def tet_left(code_ref, tet_ref, extrap_ref, low_ref, up_ref):
    pad = mm(spread(4 * FP, 4 * FW), extrap_ref[...], NT).astype(BF)
    state = tet_ref[...]
    elements = state.shape[1]
    capacity = low_ref.shape[1]
    for side, out in ((0, low_ref), (1, up_ref)):
        code = code_ref[:, side * capacity : (side + 1) * capacity]
        pick = hot(rows_of((elements, capacity)) == (code >> 2))
        columns = mm(state, pick).astype(BF)
        wide = mm(pad, columns)
        face = code & 3
        left = jnp.where(
            face < 2,
            jnp.where(face == 0, wide[:FP], wide[FP : 2 * FP]),
            jnp.where(face == 2, wide[2 * FP : 3 * FP], wide[3 * FP :]),
        )
        out[...] = left.astype(BF)


def wall_sum(prism_ref, extrap_ref, burn_ref, owner_ref, part_ref, hot_ref):
    rows = mm(extrap_ref[(NV - 1) * TFP : NV * TFP, :], prism_ref[...]).astype(BF).astype(F32)
    sums = jnp.sum(rows * rows, axis=0, keepdims=True)
    walls = burn_ref.shape[1]
    elements = prism_ref.shape[1]
    place = hot(rows_of((elements, walls)) == burn_ref[...])
    owned = hot(rows_of((8, walls)) == owner_ref[...])
    owned = mm(owned, place, NT)
    hot_ref[...] = owned
    part = jnp.sum(owned * sums, axis=1, keepdims=True)
    part_ref[...] = jnp.broadcast_to(part[None], part_ref.shape)


def tet_finish(
    count_ref, code_ref, area_ref, low_ref, up_ref, from_low_ref, from_up_ref, tet_ref, volume_ref, lift_ref, out_ref
):
    capacity = low_ref.shape[1]
    state = tet_ref[...]
    elements = state.shape[1]
    slot = cols_of((1, capacity))
    total = mm(volume_ref[...], square_half(state))
    pad = mm(lift_ref[...], spread(4 * FP, 4 * FW), NT).astype(BF)
    placed = None
    for side, own, other, normal in ((0, low_ref, from_low_ref, -1.0), (1, up_ref, from_up_ref, 1.0)):
        code = code_ref[:, side * capacity : (side + 1) * capacity]
        area = area_ref[:, side * capacity : (side + 1) * capacity]
        live = jnp.where(slot < count_ref[0, side], area, 0.0)
        left = own[...].astype(F32)
        right = other[...].astype(F32)
        speed = jnp.maximum(jnp.abs(left), jnp.abs(right))
        flux = (0.25 * normal) * (right * right - left * left) - 0.5 * speed * (right - left)
        jump = (live * flux).astype(BF)
        face = code & 3
        masked = jnp.concatenate([jnp.where(face == f, jump, jnp.zeros_like(jump)) for f in range(4)], axis=0)
        pick = hot(rows_of((elements, capacity)) == (code >> 2))
        piece = mm(masked, pick, NT)
        placed = piece if placed is None else placed + piece
    total = total + mm(pad, placed.astype(BF))
    out_ref[...] = (state.astype(F32) - STEP * total).astype(BF)


def prism_finish(parts_ref, law_ref, hot_ref, prism_ref, volume_ref, extrap_ref, lift_ref, out_ref):
    state = prism_ref[...]
    total = mm(volume_ref[...], square_half(state))
    sums = jnp.sum(parts_ref[...], axis=0)[:SECTORS]
    coef = law_ref[0, :, 0:1]
    damping = 1.0 / (1.0 + coef * sums / (BW_DEV * TFP))
    scale = coef * damping
    rows = mm(extrap_ref[...], state).astype(BF).astype(F32)
    elements = state.shape[1]
    pressure = rows[(NV - 1) * TFP :]
    squares = jnp.concatenate([pressure * pressure] * NV, axis=0)
    v = rows_of((FW, 128)) // TFP
    weight = jnp.zeros((FW, elements), F32)
    any_owner = jnp.zeros((1, elements), F32)
    for o in range(SECTORS):
        column = jnp.zeros((FW, 128), F32)
        for k in range(NV):
            gain = law_ref[0, o : o + 1, 1 + k : 2 + k] * scale[o : o + 1]
            column = jnp.where(v == k, gain, column)
        column = jnp.concatenate([column] * (elements // 128), axis=1)
        owned = hot_ref[o : o + 1, :]
        any_owner = any_owner + owned
        weight = jnp.where(owned > 0.5, column, weight)
    jump = jnp.where(any_owner > 0.5, weight * squares - rows, 0.0).astype(BF)
    total = total + mm(lift_ref[...], jump, TN)
    out_ref[...] = (state.astype(F32) - STEP * total).astype(BF)


def whole(count):
    return [pl.BlockSpec(memory_space=pltpu.VMEM)] * count


def call(kernel, name, out_shape, flops, moved, specs, *args):
    single = not isinstance(out_shape, tuple)
    return pl.pallas_call(
        kernel,
        out_shape=out_shape,
        in_specs=specs,
        out_specs=whole(1)[0] if single else tuple(whole(len(out_shape))),
        cost_estimate=pl.CostEstimate(flops=flops, bytes_accessed=moved, transcendentals=0),
        compiler_params=pltpu.CompilerParams(vmem_limit_bytes=40 * 1024 * 1024),
        name=name,
    )(*args)


def on_device(
    tet_state,
    prism_state,
    tet_volume,
    prism_volume,
    face_extrap,
    face_lift,
    wall_extrap,
    wall_lift,
    face_code,
    face_count,
    face_area,
    burn_prism,
    burn_owner,
    burn_law,
):
    slots = face_code.shape[0]
    capacity = slots // 2
    code = face_code.reshape(1, slots)
    area = face_area.reshape(1, slots)
    burn = burn_prism.reshape(1, -1)
    owner = burn_owner.reshape(1, -1)
    side = jax.ShapeDtypeStruct((FP, capacity), BF)
    low, up = call(
        tet_left, "tet_left", (side, side), 500_000_000, 600_000, whole(3), code, tet_state, face_extrap.T
    )
    count = lax.axis_size("axial")
    forward = [(i, i + 1) for i in range(count - 1)]
    backward = [(j, i) for i, j in forward]
    from_low = lax.ppermute(up, "axial", forward)
    from_up = lax.ppermute(low, "axial", backward)
    part, owned = call(
        wall_sum,
        "wall_sum",
        (
            jax.ShapeDtypeStruct((SECTORS, 8, 128), F32),
            jax.ShapeDtypeStruct((8, prism_state.shape[1]), F32),
        ),
        100_000_000,
        900_000,
        whole(4),
        prism_state,
        wall_extrap,
        burn,
        owner,
    )
    parts = lax.all_to_all(part, "azim", split_axis=0, concat_axis=0, tiled=True)
    tet_new = call(
        tet_finish,
        "tet_finish",
        jax.ShapeDtypeStruct(tet_state.shape, BF),
        800_000_000,
        1_500_000,
        [pl.BlockSpec(memory_space=pltpu.SMEM)] + whole(9),
        face_count,
        code,
        area,
        low,
        up,
        from_low,
        from_up,
        tet_state,
        tet_volume,
        face_lift,
    )
    prism_new = call(
        prism_finish,
        "prism_finish",
        jax.ShapeDtypeStruct(prism_state.shape, BF),
        400_000_000,
        2_000_000,
        whole(7),
        parts,
        burn_law,
        owned,
        prism_state,
        prism_volume,
        wall_extrap,
        wall_lift.T,
    )
    return (tet_new, prism_new)


def solution(mesh):
    elements = P(None, ("axial", "azim"))
    placed = (
        elements,
        elements,
        P(),
        P(),
        P(),
        P(),
        P(),
        P(),
        P(("axial", "azim")),
        P(("axial", "azim"), None),
        P(("axial", "azim")),
        P(("axial", "azim")),
        P(("axial", "azim"), None),
        P("axial", None, None),
    )
    return jax.shard_map(
        on_device, mesh=mesh, in_specs=placed, out_specs=(elements, elements), check_vma=False
    )
```

```python
import jax
import jax.numpy as jnp
from jax import lax
from jax.experimental import pallas as pl
from jax.experimental.pallas import tpu as pltpu
from jax.sharding import PartitionSpec as P

NV = 5
TFP = 15
FW = 75
FP = 80
BW_DEV = 512
SECTORS = 4
STEP = 0.25

BF = jnp.bfloat16
F32 = jnp.float32
NN = (((1,), (0,)), ((), ()))
NT = (((1,), (1,)), ((), ()))
TN = (((0,), (0,)), ((), ()))


def mm(a, b, dims=NN):
    return lax.dot_general(a, b, dims, preferred_element_type=F32)


def rows_of(shape):
    return lax.broadcasted_iota(jnp.int32, shape, 0)


def cols_of(shape):
    return lax.broadcasted_iota(jnp.int32, shape, 1)


def hot(mask):
    return jnp.where(mask, 1.0, 0.0).astype(BF)


def spread(rows, cols):
    r = rows_of((rows, cols))
    f = (r >= FP).astype(jnp.int32) + (r >= 2 * FP).astype(jnp.int32) + (r >= 3 * FP).astype(jnp.int32)
    c = cols_of((rows, cols))
    return hot((c == r - (FP - FW) * f) & (r - FP * f < FW))


def square_half(values):
    wide = values.astype(F32)
    return (0.5 * wide * wide).astype(BF)


def faces_of(code, state, pad):
    pick = hot(rows_of((state.shape[1], code.shape[1])) == (code >> 2))
    wide = mm(pad, mm(state, pick).astype(BF))
    face = code & 3
    return jnp.where(
        face < 2,
        jnp.where(face == 0, wide[:FP], wide[FP : 2 * FP]),
        jnp.where(face == 2, wide[2 * FP : 3 * FP], wide[3 * FP :]),
    ).astype(BF)


def load_kernel(*refs):
    loads, refs = refs[:14], refs[14:]
    (part_ref, pad_ref, owned_ref, live_ref), refs = refs[:4], refs[4:]
    (code_ref, tet_ref, prism_ref, volume_ref, prism_volume_ref, lift_ref, wall_lift_ref, wall_ref, law_ref), refs = refs[:9], refs[9:]
    burn_ref, owner_ref, extrap_ref, count_ref, area_ref, sems = refs
    targets = (
        burn_ref, owner_ref, wall_ref, extrap_ref, prism_ref, code_ref, tet_ref,
        count_ref, area_ref, law_ref, volume_ref, prism_volume_ref, lift_ref, wall_lift_ref,
    )
    copies = [pltpu.make_async_copy(a, b, sems.at[n]) for n, (a, b) in enumerate(zip(loads, targets))]
    for copy in copies:
        copy.start()
    for copy in copies[:4]:
        copy.wait()
    pad_ref[...] = mm(spread(4 * FP, 4 * FW), extrap_ref[...], NT).astype(BF)
    walls = burn_ref.shape[1]
    place = hot(rows_of((prism_ref.shape[1], walls)) == burn_ref[...])
    owned = mm(hot(rows_of((8, walls)) == owner_ref[...]), place, NT)
    owned_ref[...] = owned
    for copy in copies[4:]:
        copy.wait()
    rows = mm(wall_ref[(NV - 1) * TFP : NV * TFP, :], prism_ref[...]).astype(BF).astype(F32)
    sums = jnp.sum(rows * rows, axis=0, keepdims=True)
    part_ref[...] = jnp.broadcast_to(jnp.sum(owned * sums, axis=1, keepdims=True), part_ref.shape)
    capacity = live_ref.shape[1] // 2
    slot = cols_of((1, capacity))
    for side in range(2):
        area = area_ref[:, side * capacity : (side + 1) * capacity]
        live_ref[:, side * capacity : (side + 1) * capacity] = jnp.where(slot < count_ref[:, side : side + 1], area, 0.0)


def face_kernel(code_ref, tet_ref, pad_ref, low_ref, up_ref):
    capacity = low_ref.shape[1]
    state = tet_ref[...]
    pad = pad_ref[...]
    low_ref[...] = faces_of(code_ref[:, :capacity], state, pad)
    up_ref[...] = faces_of(code_ref[:, capacity:], state, pad)


def local_kernel(
    tet_ref, prism_ref, volume_ref, prism_volume_ref, wall_ref, lift_ref, law_ref, owned_ref,
    tet_part_ref, prism_part_ref, rows_ref, gain_ref, pad_ref,
):
    state = tet_ref[...]
    tet_part_ref[...] = state.astype(F32) - STEP * mm(volume_ref[...], square_half(state))
    pad_ref[...] = mm(lift_ref[...], spread(4 * FP, 4 * FW), NT).astype(BF)
    state = prism_ref[...]
    prism_part_ref[...] = state.astype(F32) - STEP * mm(prism_volume_ref[...], square_half(state))
    rows = mm(wall_ref[...], state).astype(BF).astype(F32)
    elements = rows.shape[1]
    pressure = rows[(NV - 1) * TFP :]
    squares = jnp.concatenate([pressure * pressure] * NV, axis=0)
    v = rows_of((FW, 128)) // TFP
    weight = jnp.zeros((FW, elements), F32)
    any_owner = jnp.zeros((1, elements), F32)
    for o in range(SECTORS):
        column = jnp.zeros((FW, 128), F32)
        for k in range(NV):
            gain = law_ref[0, o : o + 1, 1 + k : 2 + k] * law_ref[0, o : o + 1, 0:1]
            column = jnp.where(v == k, gain, column)
        column = jnp.concatenate([column] * (elements // 128), axis=1)
        owned = owned_ref[o : o + 1, :]
        any_owner = any_owner + owned
        weight = jnp.where(owned > 0.5, column, weight)
    gain_ref[...] = weight * squares
    rows_ref[...] = jnp.where(any_owner > 0.5, rows, 0.0)


def tet_kernel(code_ref, live_ref, low_ref, up_ref, from_low_ref, from_up_ref, part_ref, pad_ref, out_ref):
    capacity = low_ref.shape[1]
    elements = part_ref.shape[1]
    placed = None
    for side, own, other, normal in ((0, low_ref, from_low_ref, -1.0), (1, up_ref, from_up_ref, 1.0)):
        code = code_ref[:, side * capacity : (side + 1) * capacity]
        live = live_ref[:, side * capacity : (side + 1) * capacity]
        left = own[...].astype(F32)
        right = other[...].astype(F32)
        speed = jnp.maximum(jnp.abs(left), jnp.abs(right))
        flux = (0.25 * normal) * (right * right - left * left) - 0.5 * speed * (right - left)
        jump = (live * flux).astype(BF)
        face = code & 3
        masked = jnp.concatenate([jnp.where(face == f, jump, jnp.zeros_like(jump)) for f in range(4)], axis=0)
        pick = hot(rows_of((elements, capacity)) == (code >> 2))
        piece = mm(masked, pick, NT)
        placed = piece if placed is None else placed + piece
    out_ref[...] = (part_ref[...] - STEP * mm(pad_ref[...], placed.astype(BF))).astype(BF)


def prism_kernel(
    tet_ref, pair_ref, other_ref, law_ref, owned_ref, rows_ref, gain_ref, part_ref, lift_ref,
    tet_hbm, prism_hbm, prism_ref, sems,
):
    tet_out = pltpu.make_async_copy(tet_ref, tet_hbm, sems.at[0])
    tet_out.start()
    sums = (pair_ref[...] + other_ref[...])[:SECTORS]
    damping = 1.0 / (1.0 + law_ref[0, :, 0:1] * sums / (BW_DEV * TFP))
    elements = part_ref.shape[1]
    width = elements // 4
    lift = lift_ref[...]
    outs = []
    for n in range(4):
        at = slice(n * width, (n + 1) * width)
        factor = jnp.zeros((1, width), F32)
        for o in range(SECTORS):
            row = jnp.concatenate([damping[o : o + 1]] * (width // 128), axis=1)
            factor = jnp.where(owned_ref[o : o + 1, at] > 0.5, row, factor)
        jump = (gain_ref[:, at] * factor - rows_ref[:, at]).astype(BF)
        prism_ref[:, at] = (part_ref[:, at] - STEP * mm(lift, jump, TN)).astype(BF)
        out = pltpu.make_async_copy(prism_ref.at[:, at], prism_hbm.at[:, at], sems.at[1 + n])
        out.start()
        outs.append(out)
    for out in outs:
        out.wait()
    tet_out.wait()


VM = pl.BlockSpec(memory_space=pltpu.VMEM)
HB = pl.BlockSpec(memory_space=pltpu.HBM)


def call(kernel, name, outs, out_specs, specs, flops, moved, args, scratch=()):
    return pl.pallas_call(
        kernel,
        out_shape=outs,
        in_specs=specs,
        out_specs=out_specs,
        scratch_shapes=scratch,
        cost_estimate=pl.CostEstimate(flops=flops, bytes_accessed=moved, transcendentals=0),
        compiler_params=pltpu.CompilerParams(vmem_limit_bytes=32 * 1024 * 1024),
        name=name,
    )(*args)


def like(value):
    return pltpu.VMEM(value.shape, value.dtype)


def swap(value, axis, pairs):
    return lax.ppermute(value, axis, list(pairs) + [(j, i) for i, j in pairs])


def on_device(
    tet_state,
    prism_state,
    tet_volume,
    prism_volume,
    face_extrap,
    face_lift,
    wall_extrap,
    wall_lift,
    face_code,
    face_count,
    face_area,
    burn_prism,
    burn_owner,
    burn_law,
):
    slots = face_code.shape[0]
    capacity = slots // 2
    code = face_code.reshape(1, slots)
    area = face_area.reshape(1, slots)
    burn = burn_prism.reshape(1, -1)
    owner = burn_owner.reshape(1, -1)
    extrap = face_extrap.T
    wall_lift = wall_lift.T
    operands = (
        burn, owner, wall_extrap, extrap, prism_state, code, tet_state,
        face_count, area, burn_law, tet_volume, prism_volume, face_lift, wall_lift,
    )
    kept = (code, tet_state, prism_state, tet_volume, prism_volume, face_lift, wall_lift, wall_extrap, burn_law)
    side = pltpu.VMEM((FP, capacity), BF)
    outs = (
        pltpu.VMEM((8, 128), F32),
        pltpu.VMEM((4 * FP, tet_state.shape[0]), BF),
        pltpu.VMEM((8, prism_state.shape[1]), F32),
        pltpu.VMEM((1, slots), F32),
    ) + tuple(like(x) for x in kept)
    part, face_pad, owned, live, code, tet, prism, tet_vol, prism_vol, lift, wall_lift, wall, law = call(
        load_kernel,
        "load",
        outs,
        (VM,) * len(outs),
        [HB] * len(operands),
        5_000_000_000,
        3_000_000,
        tuple(pltpu.with_memory_space_constraint(x, pltpu.HBM) for x in operands),
        [like(x) for x in (burn, owner, extrap, face_count, area)]
        + [pltpu.SemaphoreType.DMA((len(operands),))],
    )
    half = swap(part, "azim", ((0, 1), (2, 3)))
    low, up = call(
        face_kernel, "faces", (side, side), (VM, VM), [VM] * 3, 5_000_000_000, 600_000, (code, tet, face_pad)
    )
    count = lax.axis_size("axial")
    forward = [(i, i + 1) for i in range(count - 1)]
    from_low = lax.ppermute(up, "axial", forward)
    from_up = lax.ppermute(low, "axial", [(j, i) for i, j in forward])
    pair = part + half
    other = swap(pair, "azim", ((1, 2), (0, 3)))
    pair, tet, prism = lax.optimization_barrier((pair, tet, prism))
    tet_part, prism_part, rows, gain, pad = call(
        local_kernel,
        "local",
        (
            pltpu.VMEM(tet.shape, F32),
            pltpu.VMEM(prism.shape, F32),
            pltpu.VMEM((FW, prism.shape[1]), F32),
            pltpu.VMEM((FW, prism.shape[1]), F32),
            pltpu.VMEM((tet.shape[0], 4 * FP), BF),
        ),
        (VM,) * 5,
        [VM] * 8,
        5_000_000_000,
        4_000_000,
        (tet, prism, tet_vol, prism_vol, wall, lift, law, owned),
    )
    tet_new = call(
        tet_kernel,
        "tet_finish",
        like(tet),
        VM,
        [VM] * 8,
        5_000_000_000,
        3_000_000,
        (code, live, low, up, from_low, from_up, tet_part, pad),
    )
    tet_new, prism_new = call(
        prism_kernel,
        "prism_finish",
        (jax.ShapeDtypeStruct(tet.shape, BF), jax.ShapeDtypeStruct(prism.shape, BF)),
        (HB, HB),
        [VM] * 9,
        5_000_000_000,
        3_000_000,
        (tet_new, pair, other, law, owned, rows, gain, prism_part, wall_lift),
        [like(prism), pltpu.SemaphoreType.DMA((5,))],
    )
    return (tet_new, prism_new)


def solution(mesh):
    elements = P(None, ("axial", "azim"))
    placed = (
        elements,
        elements,
        P(),
        P(),
        P(),
        P(),
        P(),
        P(),
        P(("axial", "azim")),
        P(("axial", "azim"), None),
        P(("axial", "azim")),
        P(("axial", "azim")),
        P(("axial", "azim"), None),
        P("axial", None, None),
    )
    return jax.shard_map(
        on_device, mesh=mesh, in_specs=placed, out_specs=(elements, elements), check_vma=False
    )
```

```python
import jax
import jax.numpy as jnp
from jax import lax
from jax.experimental import pallas as pl
from jax.experimental.pallas import tpu as pltpu
from jax.sharding import PartitionSpec as P

NV = 5
TFP = 15
FW = 75
FP = 80
BW_DEV = 512
SECTORS = 4
STEP = 0.25

BF = jnp.bfloat16
F32 = jnp.float32
NN = (((1,), (0,)), ((), ()))
NT = (((1,), (1,)), ((), ()))
TN = (((0,), (0,)), ((), ()))


def mm(a, b, dims=NN):
    return lax.dot_general(a, b, dims, preferred_element_type=F32)


def rows_of(shape):
    return lax.broadcasted_iota(jnp.int32, shape, 0)


def cols_of(shape):
    return lax.broadcasted_iota(jnp.int32, shape, 1)


def hot(mask):
    return jnp.where(mask, 1.0, 0.0).astype(BF)


def spread(rows, cols):
    r = rows_of((rows, cols))
    f = (r >= FP).astype(jnp.int32) + (r >= 2 * FP).astype(jnp.int32) + (r >= 3 * FP).astype(jnp.int32)
    c = cols_of((rows, cols))
    return hot((c == r - (FP - FW) * f) & (r - FP * f < FW))


def square_half(values):
    wide = values.astype(F32)
    return (0.5 * wide * wide).astype(BF)


def faces_of(code, state, pad):
    pick = hot(rows_of((state.shape[1], code.shape[1])) == (code >> 2))
    wide = mm(pad, mm(state, pick).astype(BF))
    face = code & 3
    return jnp.where(
        face < 2,
        jnp.where(face == 0, wide[:FP], wide[FP : 2 * FP]),
        jnp.where(face == 2, wide[2 * FP : 3 * FP], wide[3 * FP :]),
    ).astype(BF)


def first_side():
    return 1 - (lax.axis_index("axial") & 1)


def side_of(ref, side):
    width = ref.shape[1] // 2
    return ref[:, pl.ds(pl.multiple_of(side * width, width), width)]


def send_kernel(
    code_hbm, burn_hbm, owner_hbm, extrap_hbm, wall_hbm, tet_hbm, prism_hbm,
    part_ref, odd_ref, even_ref, owned_ref, code_ref, wall_ref, tet_ref, prism_ref,
    burn_ref, owner_ref, extrap_ref, sems,
):
    pairs = (
        (code_hbm, code_ref), (burn_hbm, burn_ref), (owner_hbm, owner_ref), (extrap_hbm, extrap_ref),
        (wall_hbm, wall_ref), (tet_hbm, tet_ref), (prism_hbm, prism_ref),
    )
    copies = [pltpu.make_async_copy(a, b, sems.at[n]) for n, (a, b) in enumerate(pairs)]
    for copy in copies:
        copy.start()
    spreads = spread(4 * FP, 4 * FW)
    for copy in copies[:4]:
        copy.wait()
    pad = mm(spreads, extrap_ref[...], NT).astype(BF)
    walls = burn_ref.shape[1]
    place = hot(rows_of((prism_ref.shape[1], walls)) == burn_ref[...])
    owned = mm(hot(rows_of((8, walls)) == owner_ref[...]), place, NT)
    owned_ref[...] = owned
    for copy in copies[4:]:
        copy.wait()
    capacity = odd_ref.shape[1]
    left = faces_of(code_ref[...], tet_ref[...], pad)
    upper = first_side() == 1
    odd_ref[...] = jnp.where(upper, left[:, :capacity], left[:, capacity:])
    even_ref[...] = jnp.where(upper, left[:, capacity:], left[:, :capacity])
    rows = mm(wall_ref[(NV - 1) * TFP : NV * TFP, :], prism_ref[...]).astype(BF).astype(F32)
    sums = jnp.sum(rows * rows, axis=0, keepdims=True)
    part_ref[...] = jnp.broadcast_to(jnp.sum(owned * sums, axis=1, keepdims=True), part_ref.shape)


def local_kernel(
    tet_ref, prism_ref, wall_ref, owned_ref, volume_hbm, prism_volume_hbm, lift_hbm, law_hbm, wall_lift_hbm, count_hbm, area_hbm,
    tet_part_ref, prism_part_ref, rows_ref, gain_ref, pad_ref, live_ref, law_ref, wall_lift_ref,
    volume_ref, prism_volume_ref, lift_ref, count_ref, area_ref, sems,
):
    pairs = (
        (law_hbm, law_ref), (prism_volume_hbm, prism_volume_ref), (volume_hbm, volume_ref), (lift_hbm, lift_ref),
        (count_hbm, count_ref), (area_hbm, area_ref), (wall_lift_hbm, wall_lift_ref),
    )
    copies = [pltpu.make_async_copy(a, b, sems.at[n]) for n, (a, b) in enumerate(pairs)]
    for copy in copies:
        copy.start()
    rows = mm(wall_ref[...], prism_ref[...]).astype(BF).astype(F32)
    elements = rows.shape[1]
    any_owner = jnp.sum(owned_ref[:SECTORS, :], axis=0, keepdims=True)
    rows_ref[...] = jnp.where(any_owner > 0.5, rows, 0.0)
    pressure = rows[(NV - 1) * TFP :]
    squares = jnp.concatenate([pressure * pressure] * NV, axis=0)
    for copy in copies:
        copy.wait()
    v = rows_of((FW, 128)) // TFP
    weight = jnp.zeros((FW, elements), F32)
    for o in range(SECTORS):
        column = jnp.zeros((FW, 128), F32)
        for k in range(NV):
            gain = law_ref[0, o : o + 1, 1 + k : 2 + k] * law_ref[0, o : o + 1, 0:1]
            column = jnp.where(v == k, gain, column)
        column = jnp.concatenate([column] * (elements // 128), axis=1)
        weight = jnp.where(owned_ref[o : o + 1, :] > 0.5, column, weight)
    gain_ref[...] = weight * squares
    state = prism_ref[...]
    prism_part_ref[...] = state.astype(F32) - STEP * mm(prism_volume_ref[...], square_half(state))
    state = tet_ref[...]
    tet_part_ref[...] = state.astype(F32) - STEP * mm(volume_ref[...], square_half(state))
    pad_ref[...] = mm(lift_ref[...], spread(4 * FP, 4 * FW), NT).astype(BF)
    capacity = live_ref.shape[1] // 2
    slot = cols_of((1, capacity))
    for side in range(2):
        area = area_ref[:, side * capacity : (side + 1) * capacity]
        live_ref[:, side * capacity : (side + 1) * capacity] = jnp.where(slot < count_ref[:, side : side + 1], area, 0.0)


def tet_kernel(code_ref, live_ref, odd_ref, even_ref, from_odd_ref, from_even_ref, part_ref, pad_ref, out_ref):
    first = first_side()
    capacity = even_ref.shape[1]
    elements = part_ref.shape[1]
    placed = None
    for side, own, other in ((1 - first, odd_ref, from_odd_ref), (first, even_ref, from_even_ref)):
        code = side_of(code_ref, side)
        live = side_of(live_ref, side)
        normal = jnp.where(side == 0, -0.25, 0.25)
        left = own[...].astype(F32)
        right = other[...].astype(F32)
        speed = jnp.maximum(jnp.abs(left), jnp.abs(right))
        flux = normal * (right * right - left * left) - 0.5 * speed * (right - left)
        jump = (live * flux).astype(BF)
        face = code & 3
        masked = jnp.concatenate([jnp.where(face == f, jump, jnp.zeros_like(jump)) for f in range(4)], axis=0)
        pick = hot(rows_of((elements, capacity)) == (code >> 2))
        piece = mm(masked, pick, NT)
        placed = piece if placed is None else placed + piece
    out_ref[...] = (part_ref[...] - STEP * mm(pad_ref[...], placed.astype(BF))).astype(BF)


def prism_kernel(
    tet_ref, pair_ref, other_ref, law_ref, owned_ref, rows_ref, gain_ref, part_ref, lift_ref,
    tet_hbm, prism_hbm, prism_ref, sems,
):
    tet_out = pltpu.make_async_copy(tet_ref, tet_hbm, sems.at[0])
    tet_out.start()
    sums = (pair_ref[...] + other_ref[...])[:SECTORS]
    damping = 1.0 / (1.0 + law_ref[0, :, 0:1] * sums / (BW_DEV * TFP))
    elements = part_ref.shape[1]
    width = elements // 4
    lift = lift_ref[...]
    outs = []
    for n in range(4):
        at = slice(n * width, (n + 1) * width)
        factor = jnp.zeros((1, width), F32)
        for o in range(SECTORS):
            row = jnp.concatenate([damping[o : o + 1]] * (width // 128), axis=1)
            factor = jnp.where(owned_ref[o : o + 1, at] > 0.5, row, factor)
        jump = (gain_ref[:, at] * factor - rows_ref[:, at]).astype(BF)
        prism_ref[:, at] = (part_ref[:, at] - STEP * mm(lift, jump, TN)).astype(BF)
        out = pltpu.make_async_copy(prism_ref.at[:, at], prism_hbm.at[:, at], sems.at[1 + n])
        out.start()
        outs.append(out)
    for out in outs:
        out.wait()
    tet_out.wait()


VM = pl.BlockSpec(memory_space=pltpu.VMEM)
HB = pl.BlockSpec(memory_space=pltpu.HBM)


def call(kernel, name, outs, out_specs, specs, flops, moved, args, scratch=()):
    return pl.pallas_call(
        kernel,
        out_shape=outs,
        in_specs=specs,
        out_specs=out_specs,
        scratch_shapes=scratch,
        cost_estimate=pl.CostEstimate(flops=flops, bytes_accessed=moved, transcendentals=0),
        compiler_params=pltpu.CompilerParams(vmem_limit_bytes=32 * 1024 * 1024),
        name=name,
    )(*args)


def like(value):
    return pltpu.VMEM(value.shape, value.dtype)


def swap(value, axis, pairs):
    return lax.ppermute(value, axis, list(pairs) + [(j, i) for i, j in pairs])


def on_device(
    tet_state,
    prism_state,
    tet_volume,
    prism_volume,
    face_extrap,
    face_lift,
    wall_extrap,
    wall_lift,
    face_code,
    face_count,
    face_area,
    burn_prism,
    burn_owner,
    burn_law,
):
    slots = face_code.shape[0]
    capacity = slots // 2
    code = face_code.reshape(1, slots)
    area = face_area.reshape(1, slots)
    burn = burn_prism.reshape(1, -1)
    owner = burn_owner.reshape(1, -1)
    extrap = face_extrap.T
    wall_lift = wall_lift.T
    tall = prism_state.shape[1]
    side = pltpu.VMEM((FP, capacity), BF)
    hbm = pltpu.with_memory_space_constraint
    operands = (code, burn, owner, extrap, wall_extrap, tet_state, prism_state)
    part, odd, even, owned, code, wall, tet, prism = call(
        send_kernel,
        "send",
        (pltpu.VMEM((8, 128), F32), side, side, pltpu.VMEM((8, tall), F32))
        + tuple(like(x) for x in (code, wall_extrap, tet_state, prism_state)),
        (VM,) * 8,
        [HB] * 7,
        5_000_000_000,
        3_000_000,
        tuple(hbm(x, pltpu.HBM) for x in operands),
        [like(x) for x in (burn, owner, extrap)] + [pltpu.SemaphoreType.DMA((7,))],
    )
    half = swap(part, "azim", ((0, 1), (2, 3)))
    count = lax.axis_size("axial")
    from_even = swap(even, "axial", [(i, i + 1) for i in range(0, count - 1, 2)])
    from_odd = swap(odd, "axial", [(i, i + 1) for i in range(1, count - 1, 2)])
    pair = part + half
    other = swap(pair, "azim", ((1, 2), (0, 3)))
    pair, tet, prism = lax.optimization_barrier((pair, tet, prism))
    operands = (tet_volume, prism_volume, face_lift, burn_law, wall_lift, face_count, area)
    tet_part, prism_part, rows, gain, pad, live, law, wall_lift = call(
        local_kernel,
        "local",
        (
            pltpu.VMEM(tet.shape, F32),
            pltpu.VMEM(prism.shape, F32),
            pltpu.VMEM((FW, tall), F32),
            pltpu.VMEM((FW, tall), F32),
            pltpu.VMEM((tet.shape[0], 4 * FP), BF),
            like(area),
            like(burn_law),
            like(wall_lift),
        ),
        (VM,) * 8,
        [VM] * 4 + [HB] * 7,
        5_000_000_000,
        4_000_000,
        (tet, prism, wall, owned) + tuple(hbm(x, pltpu.HBM) for x in operands),
        [like(x) for x in (tet_volume, prism_volume, face_lift, face_count, area)]
        + [pltpu.SemaphoreType.DMA((7,))],
    )
    tet_new = call(
        tet_kernel,
        "tet_finish",
        like(tet),
        VM,
        [VM] * 8,
        5_000_000_000,
        3_000_000,
        (code, live, odd, even, from_odd, from_even, tet_part, pad),
    )
    tet_new, prism_new = call(
        prism_kernel,
        "prism_finish",
        (jax.ShapeDtypeStruct(tet.shape, BF), jax.ShapeDtypeStruct(prism.shape, BF)),
        (HB, HB),
        [VM] * 9,
        5_000_000_000,
        3_000_000,
        (tet_new, pair, other, law, owned, rows, gain, prism_part, wall_lift),
        [like(prism), pltpu.SemaphoreType.DMA((5,))],
    )
    return (tet_new, prism_new)


def solution(mesh):
    elements = P(None, ("axial", "azim"))
    placed = (
        elements,
        elements,
        P(),
        P(),
        P(),
        P(),
        P(),
        P(),
        P(("axial", "azim")),
        P(("axial", "azim"), None),
        P(("axial", "azim")),
        P(("axial", "azim")),
        P(("axial", "azim"), None),
        P("axial", None, None),
    )
    return jax.shard_map(
        on_device, mesh=mesh, in_specs=placed, out_specs=(elements, elements), check_vma=False
    )
```

```python
import jax
import jax.numpy as jnp
from jax import lax
from jax.experimental import pallas as pl
from jax.experimental.pallas import tpu as pltpu
from jax.sharding import PartitionSpec as P

NV = 5
TFP = 15
FW = 75
FP = 80
BW_DEV = 512
SECTORS = 4
STEP = 0.25

BF = jnp.bfloat16
F32 = jnp.float32
NN = (((1,), (0,)), ((), ()))
NT = (((1,), (1,)), ((), ()))
TN = (((0,), (0,)), ((), ()))


def mm(a, b, dims=NN):
    return lax.dot_general(a, b, dims, preferred_element_type=F32)


def rows_of(shape):
    return lax.broadcasted_iota(jnp.int32, shape, 0)


def cols_of(shape):
    return lax.broadcasted_iota(jnp.int32, shape, 1)


def hot(mask):
    return jnp.where(mask, 1.0, 0.0).astype(BF)


def spread(rows, cols):
    r = rows_of((rows, cols))
    f = (r >= FP).astype(jnp.int32) + (r >= 2 * FP).astype(jnp.int32) + (r >= 3 * FP).astype(jnp.int32)
    c = cols_of((rows, cols))
    return hot((c == r - (FP - FW) * f) & (r - FP * f < FW))


def square_half(values):
    wide = values.astype(F32)
    return (0.5 * wide * wide).astype(BF)


def faces_of(code, state, pad):
    pick = hot(rows_of((state.shape[1], code.shape[1])) == (code >> 2))
    wide = mm(pad, mm(state, pick).astype(BF))
    face = code & 3
    return jnp.where(
        face < 2,
        jnp.where(face == 0, wide[:FP], wide[FP : 2 * FP]),
        jnp.where(face == 2, wide[2 * FP : 3 * FP], wide[3 * FP :]),
    ).astype(BF)


def first_side():
    return 1 - (lax.axis_index("axial") & 1)


def side_of(ref, side):
    width = ref.shape[1] // 2
    return ref[:, pl.ds(pl.multiple_of(side * width, width), width)]


def wall_kernel(
    burn_hbm, owner_hbm, wall_hbm, prism_hbm, extrap_hbm, code_hbm, tet_hbm,
    part_ref, pad_ref, owned_ref, code_ref, wall_ref, tet_ref, prism_ref,
    burn_ref, owner_ref, extrap_ref, sems,
):
    pairs = (
        (burn_hbm, burn_ref), (owner_hbm, owner_ref), (wall_hbm, wall_ref), (extrap_hbm, extrap_ref),
        (prism_hbm, prism_ref), (code_hbm, code_ref), (tet_hbm, tet_ref),
    )
    copies = [pltpu.make_async_copy(a, b, sems.at[n]) for n, (a, b) in enumerate(pairs)]
    for copy in copies:
        copy.start()
    spreads = spread(4 * FP, 4 * FW)
    for copy in copies[:4]:
        copy.wait()
    pad_ref[...] = mm(spreads, extrap_ref[...], NT).astype(BF)
    walls = burn_ref.shape[1]
    place = hot(rows_of((prism_ref.shape[1], walls)) == burn_ref[...])
    owned = mm(hot(rows_of((8, walls)) == owner_ref[...]), place, NT)
    owned_ref[...] = owned
    for copy in copies[4:]:
        copy.wait()
    rows = mm(wall_ref[(NV - 1) * TFP : NV * TFP, :], prism_ref[...]).astype(BF).astype(F32)
    sums = jnp.sum(rows * rows, axis=0, keepdims=True)
    part_ref[...] = jnp.broadcast_to(jnp.sum(owned * sums, axis=1, keepdims=True), part_ref.shape)


def face_kernel(code_ref, tet_ref, pad_ref, odd_ref, even_ref):
    capacity = odd_ref.shape[1]
    left = faces_of(code_ref[...], tet_ref[...], pad_ref[...])
    upper = first_side() == 1
    odd_ref[...] = jnp.where(upper, left[:, :capacity], left[:, capacity:])
    even_ref[...] = jnp.where(upper, left[:, capacity:], left[:, :capacity])


def local_kernel(
    tet_ref, prism_ref, wall_ref, owned_ref, volume_ref, prism_volume_ref, lift_ref, law_ref, count_ref, area_ref,
    tet_part_ref, prism_part_ref, rows_ref, gain_ref, pad_ref, live_ref,
):
    rows = mm(wall_ref[...], prism_ref[...]).astype(BF).astype(F32)
    elements = rows.shape[1]
    any_owner = jnp.sum(owned_ref[:SECTORS, :], axis=0, keepdims=True)
    rows_ref[...] = jnp.where(any_owner > 0.5, rows, 0.0)
    pressure = rows[(NV - 1) * TFP :]
    squares = jnp.concatenate([pressure * pressure] * NV, axis=0)
    v = rows_of((FW, 128)) // TFP
    weight = jnp.zeros((FW, elements), F32)
    for o in range(SECTORS):
        column = jnp.zeros((FW, 128), F32)
        for k in range(NV):
            gain = law_ref[0, o : o + 1, 1 + k : 2 + k] * law_ref[0, o : o + 1, 0:1]
            column = jnp.where(v == k, gain, column)
        column = jnp.concatenate([column] * (elements // 128), axis=1)
        weight = jnp.where(owned_ref[o : o + 1, :] > 0.5, column, weight)
    gain_ref[...] = weight * squares
    state = prism_ref[...]
    prism_part_ref[...] = state.astype(F32) - STEP * mm(prism_volume_ref[...], square_half(state))
    state = tet_ref[...]
    tet_part_ref[...] = state.astype(F32) - STEP * mm(volume_ref[...], square_half(state))
    pad_ref[...] = mm(lift_ref[...], spread(4 * FP, 4 * FW), NT).astype(BF)
    capacity = live_ref.shape[1] // 2
    slot = cols_of((1, capacity))
    for side in range(2):
        area = area_ref[:, side * capacity : (side + 1) * capacity]
        live_ref[:, side * capacity : (side + 1) * capacity] = jnp.where(slot < count_ref[:, side : side + 1], area, 0.0)


def tet_kernel(code_ref, live_ref, odd_ref, even_ref, from_odd_ref, from_even_ref, part_ref, pad_ref, out_ref):
    first = first_side()
    capacity = even_ref.shape[1]
    elements = part_ref.shape[1]
    placed = None
    for side, own, other in ((1 - first, odd_ref, from_odd_ref), (first, even_ref, from_even_ref)):
        code = side_of(code_ref, side)
        live = side_of(live_ref, side)
        normal = jnp.where(side == 0, -0.25, 0.25)
        left = own[...].astype(F32)
        right = other[...].astype(F32)
        speed = jnp.maximum(jnp.abs(left), jnp.abs(right))
        flux = normal * (right * right - left * left) - 0.5 * speed * (right - left)
        jump = (live * flux).astype(BF)
        face = code & 3
        masked = jnp.concatenate([jnp.where(face == f, jump, jnp.zeros_like(jump)) for f in range(4)], axis=0)
        pick = hot(rows_of((elements, capacity)) == (code >> 2))
        piece = mm(masked, pick, NT)
        placed = piece if placed is None else placed + piece
    out_ref[...] = (part_ref[...] - STEP * mm(pad_ref[...], placed.astype(BF))).astype(BF)


def prism_kernel(
    tet_ref, pair_ref, other_ref, law_ref, owned_ref, rows_ref, gain_ref, part_ref, lift_ref,
    tet_hbm, prism_hbm, prism_ref, sems,
):
    tet_out = pltpu.make_async_copy(tet_ref, tet_hbm, sems.at[0])
    tet_out.start()
    sums = (pair_ref[...] + other_ref[...])[:SECTORS]
    damping = 1.0 / (1.0 + law_ref[0, :, 0:1] * sums / (BW_DEV * TFP))
    elements = part_ref.shape[1]
    width = elements // 4
    lift = lift_ref[...]
    outs = []
    for n in range(4):
        at = slice(n * width, (n + 1) * width)
        factor = jnp.zeros((1, width), F32)
        for o in range(SECTORS):
            row = jnp.concatenate([damping[o : o + 1]] * (width // 128), axis=1)
            factor = jnp.where(owned_ref[o : o + 1, at] > 0.5, row, factor)
        jump = (gain_ref[:, at] * factor - rows_ref[:, at]).astype(BF)
        prism_ref[:, at] = (part_ref[:, at] - STEP * mm(lift, jump, TN)).astype(BF)
        out = pltpu.make_async_copy(prism_ref.at[:, at], prism_hbm.at[:, at], sems.at[1 + n])
        out.start()
        outs.append(out)
    for out in outs:
        out.wait()
    tet_out.wait()


VM = pl.BlockSpec(memory_space=pltpu.VMEM)
HB = pl.BlockSpec(memory_space=pltpu.HBM)


def call(kernel, name, outs, out_specs, specs, flops, moved, args, scratch=()):
    return pl.pallas_call(
        kernel,
        out_shape=outs,
        in_specs=specs,
        out_specs=out_specs,
        scratch_shapes=scratch,
        cost_estimate=pl.CostEstimate(flops=flops, bytes_accessed=moved, transcendentals=0),
        compiler_params=pltpu.CompilerParams(vmem_limit_bytes=32 * 1024 * 1024),
        name=name,
    )(*args)


def like(value):
    return pltpu.VMEM(value.shape, value.dtype)


def swap(value, axis, pairs):
    return lax.ppermute(value, axis, list(pairs) + [(j, i) for i, j in pairs])


def on_device(
    tet_state,
    prism_state,
    tet_volume,
    prism_volume,
    face_extrap,
    face_lift,
    wall_extrap,
    wall_lift,
    face_code,
    face_count,
    face_area,
    burn_prism,
    burn_owner,
    burn_law,
):
    slots = face_code.shape[0]
    capacity = slots // 2
    code = face_code.reshape(1, slots)
    area = face_area.reshape(1, slots)
    burn = burn_prism.reshape(1, -1)
    owner = burn_owner.reshape(1, -1)
    extrap = face_extrap.T
    wall_lift = wall_lift.T
    tall = prism_state.shape[1]
    side = pltpu.VMEM((FP, capacity), BF)
    hbm = pltpu.with_memory_space_constraint
    operands = (burn, owner, wall_extrap, prism_state, extrap, code, tet_state)
    part, face_pad, owned, code, wall, tet, prism = call(
        wall_kernel,
        "walls",
        (
            pltpu.VMEM((8, 128), F32),
            pltpu.VMEM((4 * FP, tet_state.shape[0]), BF),
            pltpu.VMEM((8, tall), F32),
        )
        + tuple(like(x) for x in (code, wall_extrap, tet_state, prism_state)),
        (VM,) * 7,
        [HB] * 7,
        5_000_000_000,
        3_000_000,
        tuple(hbm(x, pltpu.HBM) for x in operands),
        [like(x) for x in (burn, owner, extrap)] + [pltpu.SemaphoreType.DMA((7,))],
    )
    odd, even = call(
        face_kernel, "faces", (side, side), (VM, VM), [VM] * 3, 5_000_000_000, 600_000, (code, tet, face_pad)
    )
    part, tet_volume, prism_volume, face_lift, wall_lift, law, face_count, area = lax.optimization_barrier(
        (part, tet_volume, prism_volume, face_lift, wall_lift, burn_law, face_count, area)
    )
    half = swap(part, "azim", ((0, 3), (1, 2)))
    count = lax.axis_size("axial")
    from_even = swap(even, "axial", [(i, i + 1) for i in range(0, count - 1, 2)])
    from_odd = swap(odd, "axial", [(i, i + 1) for i in range(1, count - 1, 2)])
    pair = part + half
    other = swap(pair, "azim", ((0, 1), (2, 3)))
    pair, tet, prism = lax.optimization_barrier((pair, tet, prism))
    tet_part, prism_part, rows, gain, pad, live = call(
        local_kernel,
        "local",
        (
            pltpu.VMEM(tet.shape, F32),
            pltpu.VMEM(prism.shape, F32),
            pltpu.VMEM((FW, tall), F32),
            pltpu.VMEM((FW, tall), F32),
            pltpu.VMEM((tet.shape[0], 4 * FP), BF),
            like(area),
        ),
        (VM,) * 6,
        [VM] * 10,
        5_000_000_000,
        4_000_000,
        (tet, prism, wall, owned, tet_volume, prism_volume, face_lift, law, face_count, area),
    )
    tet_new = call(
        tet_kernel,
        "tet_finish",
        like(tet),
        VM,
        [VM] * 8,
        5_000_000_000,
        3_000_000,
        (code, live, odd, even, from_odd, from_even, tet_part, pad),
    )
    tet_new, prism_new = call(
        prism_kernel,
        "prism_finish",
        (jax.ShapeDtypeStruct(tet.shape, BF), jax.ShapeDtypeStruct(prism.shape, BF)),
        (HB, HB),
        [VM] * 9,
        5_000_000_000,
        3_000_000,
        (tet_new, pair, other, law, owned, rows, gain, prism_part, wall_lift),
        [like(prism), pltpu.SemaphoreType.DMA((5,))],
    )
    return (tet_new, prism_new)


def solution(mesh):
    elements = P(None, ("axial", "azim"))
    placed = (
        elements,
        elements,
        P(),
        P(),
        P(),
        P(),
        P(),
        P(),
        P(("axial", "azim")),
        P(("axial", "azim"), None),
        P(("axial", "azim")),
        P(("axial", "azim")),
        P(("axial", "azim"), None),
        P("axial", None, None),
    )
    return jax.shard_map(
        on_device, mesh=mesh, in_specs=placed, out_specs=(elements, elements), check_vma=False
    )
```

```python
import jax
import jax.numpy as jnp
from jax import lax
from jax.experimental import pallas as pl
from jax.experimental.pallas import tpu as pltpu
from jax.sharding import PartitionSpec as P

NV = 5
TFP = 15
FW = 75
FP = 80
BW_DEV = 512
SECTORS = 4
STEP = 0.25

BF = jnp.bfloat16
F32 = jnp.float32
NN = (((1,), (0,)), ((), ()))
NT = (((1,), (1,)), ((), ()))
TN = (((0,), (0,)), ((), ()))


def mm(a, b, dims=NN):
    return lax.dot_general(a, b, dims, preferred_element_type=F32)


def rows_of(shape):
    return lax.broadcasted_iota(jnp.int32, shape, 0)


def cols_of(shape):
    return lax.broadcasted_iota(jnp.int32, shape, 1)


def hot(mask):
    return jnp.where(mask, 1.0, 0.0).astype(BF)


def spread(rows, cols):
    r = rows_of((rows, cols))
    f = (r >= FP).astype(jnp.int32) + (r >= 2 * FP).astype(jnp.int32) + (r >= 3 * FP).astype(jnp.int32)
    c = cols_of((rows, cols))
    return hot((c == r - (FP - FW) * f) & (r - FP * f < FW))


def square_half(values):
    wide = values.astype(F32)
    return (0.5 * wide * wide).astype(BF)


def faces_of(code, state, pad):
    pick = hot(rows_of((state.shape[1], code.shape[1])) == (code >> 2))
    wide = mm(pad, mm(state, pick).astype(BF))
    face = code & 3
    return jnp.where(
        face < 2,
        jnp.where(face == 0, wide[:FP], wide[FP : 2 * FP]),
        jnp.where(face == 2, wide[2 * FP : 3 * FP], wide[3 * FP :]),
    ).astype(BF)


def first_side():
    return 1 - (lax.axis_index("axial") & 1)


def side_of(ref, side):
    width = ref.shape[1] // 2
    return ref[:, pl.ds(pl.multiple_of(side * width, width), width)]


def wall_kernel(
    burn_hbm, owner_hbm, prism_hbm, wall_hbm, tet_hbm, code_hbm, extrap_hbm,
    part_ref, owned_ref, prism_ref, wall_ref, tet_ref, code_ref, extrap_ref,
    burn_ref, owner_ref, sems,
):
    pairs = (
        (burn_hbm, burn_ref), (owner_hbm, owner_ref), (prism_hbm, prism_ref), (wall_hbm, wall_ref),
        (tet_hbm, tet_ref), (code_hbm, code_ref), (extrap_hbm, extrap_ref),
    )
    copies = [pltpu.make_async_copy(a, b, sems.at[n]) for n, (a, b) in enumerate(pairs)]
    for copy in copies:
        copy.start()
    for copy in copies[:2]:
        copy.wait()
    walls = burn_ref.shape[1]
    place = hot(rows_of((prism_ref.shape[1], walls)) == burn_ref[...])
    owned = mm(hot(rows_of((8, walls)) == owner_ref[...]), place, NT)
    owned_ref[...] = owned
    for copy in copies[2:4]:
        copy.wait()
    rows = mm(wall_ref[(NV - 1) * TFP : NV * TFP, :], prism_ref[...]).astype(BF).astype(F32)
    sums = jnp.sum(rows * rows, axis=0, keepdims=True)
    part_ref[...] = jnp.broadcast_to(jnp.sum(owned * sums, axis=1, keepdims=True), part_ref.shape)
    for copy in copies[4:]:
        copy.wait()


def face_kernel(code_ref, tet_ref, extrap_ref, odd_ref, even_ref):
    capacity = odd_ref.shape[1]
    pad = mm(spread(4 * FP, 4 * FW), extrap_ref[...], NT).astype(BF)
    left = faces_of(code_ref[...], tet_ref[...], pad)
    upper = first_side() == 1
    odd_ref[...] = jnp.where(upper, left[:, :capacity], left[:, capacity:])
    even_ref[...] = jnp.where(upper, left[:, capacity:], left[:, :capacity])


def local_kernel(
    tet_ref, prism_ref, wall_ref, owned_ref, volume_ref, prism_volume_ref, lift_ref, law_ref, count_ref, area_ref,
    tet_part_ref, prism_part_ref, rows_ref, gain_ref, pad_ref, live_ref,
):
    rows = mm(wall_ref[...], prism_ref[...]).astype(BF).astype(F32)
    elements = rows.shape[1]
    any_owner = jnp.sum(owned_ref[:SECTORS, :], axis=0, keepdims=True)
    rows_ref[...] = jnp.where(any_owner > 0.5, rows, 0.0)
    pressure = rows[(NV - 1) * TFP :]
    squares = jnp.concatenate([pressure * pressure] * NV, axis=0)
    v = rows_of((FW, 128)) // TFP
    weight = jnp.zeros((FW, elements), F32)
    for o in range(SECTORS):
        column = jnp.zeros((FW, 128), F32)
        for k in range(NV):
            gain = law_ref[0, o : o + 1, 1 + k : 2 + k] * law_ref[0, o : o + 1, 0:1]
            column = jnp.where(v == k, gain, column)
        column = jnp.concatenate([column] * (elements // 128), axis=1)
        weight = jnp.where(owned_ref[o : o + 1, :] > 0.5, column, weight)
    gain_ref[...] = weight * squares
    state = prism_ref[...]
    prism_part_ref[...] = state.astype(F32) - STEP * mm(prism_volume_ref[...], square_half(state))
    state = tet_ref[...]
    tet_part_ref[...] = state.astype(F32) - STEP * mm(volume_ref[...], square_half(state))
    pad_ref[...] = mm(lift_ref[...], spread(4 * FP, 4 * FW), NT).astype(BF)
    capacity = live_ref.shape[1] // 2
    slot = cols_of((1, capacity))
    for side in range(2):
        area = area_ref[:, side * capacity : (side + 1) * capacity]
        live_ref[:, side * capacity : (side + 1) * capacity] = jnp.where(slot < count_ref[:, side : side + 1], area, 0.0)


def tet_kernel(code_ref, live_ref, odd_ref, even_ref, from_odd_ref, from_even_ref, part_ref, pad_ref, out_ref):
    first = first_side()
    capacity = even_ref.shape[1]
    elements = part_ref.shape[1]
    placed = None
    for side, own, other in ((1 - first, odd_ref, from_odd_ref), (first, even_ref, from_even_ref)):
        code = side_of(code_ref, side)
        live = side_of(live_ref, side)
        normal = jnp.where(side == 0, -0.25, 0.25)
        left = own[...].astype(F32)
        right = other[...].astype(F32)
        speed = jnp.maximum(jnp.abs(left), jnp.abs(right))
        flux = normal * (right * right - left * left) - 0.5 * speed * (right - left)
        jump = (live * flux).astype(BF)
        face = code & 3
        masked = jnp.concatenate([jnp.where(face == f, jump, jnp.zeros_like(jump)) for f in range(4)], axis=0)
        pick = hot(rows_of((elements, capacity)) == (code >> 2))
        piece = mm(masked, pick, NT)
        placed = piece if placed is None else placed + piece
    out_ref[...] = (part_ref[...] - STEP * mm(pad_ref[...], placed.astype(BF))).astype(BF)


def prism_kernel(
    tet_ref, pair_ref, other_ref, law_ref, owned_ref, rows_ref, gain_ref, part_ref, lift_ref,
    tet_hbm, prism_hbm, prism_ref, sems,
):
    tet_out = pltpu.make_async_copy(tet_ref, tet_hbm, sems.at[0])
    tet_out.start()
    sums = (pair_ref[...] + other_ref[...])[:SECTORS]
    damping = 1.0 / (1.0 + law_ref[0, :, 0:1] * sums / (BW_DEV * TFP))
    elements = part_ref.shape[1]
    width = elements // 4
    lift = lift_ref[...]
    outs = []
    for n in range(4):
        at = slice(n * width, (n + 1) * width)
        factor = jnp.zeros((1, width), F32)
        for o in range(SECTORS):
            row = jnp.concatenate([damping[o : o + 1]] * (width // 128), axis=1)
            factor = jnp.where(owned_ref[o : o + 1, at] > 0.5, row, factor)
        jump = (gain_ref[:, at] * factor - rows_ref[:, at]).astype(BF)
        prism_ref[:, at] = (part_ref[:, at] - STEP * mm(lift, jump, TN)).astype(BF)
        out = pltpu.make_async_copy(prism_ref.at[:, at], prism_hbm.at[:, at], sems.at[1 + n])
        out.start()
        outs.append(out)
    for out in outs:
        out.wait()
    tet_out.wait()


VM = pl.BlockSpec(memory_space=pltpu.VMEM)
HB = pl.BlockSpec(memory_space=pltpu.HBM)


def call(kernel, name, outs, out_specs, specs, flops, moved, args, scratch=()):
    return pl.pallas_call(
        kernel,
        out_shape=outs,
        in_specs=specs,
        out_specs=out_specs,
        scratch_shapes=scratch,
        cost_estimate=pl.CostEstimate(flops=flops, bytes_accessed=moved, transcendentals=0),
        compiler_params=pltpu.CompilerParams(vmem_limit_bytes=32 * 1024 * 1024),
        name=name,
    )(*args)


def like(value):
    return pltpu.VMEM(value.shape, value.dtype)


def swap(value, axis, pairs):
    return lax.ppermute(value, axis, list(pairs) + [(j, i) for i, j in pairs])


def on_device(
    tet_state,
    prism_state,
    tet_volume,
    prism_volume,
    face_extrap,
    face_lift,
    wall_extrap,
    wall_lift,
    face_code,
    face_count,
    face_area,
    burn_prism,
    burn_owner,
    burn_law,
):
    slots = face_code.shape[0]
    capacity = slots // 2
    code = face_code.reshape(1, slots)
    area = face_area.reshape(1, slots)
    burn = burn_prism.reshape(1, -1)
    owner = burn_owner.reshape(1, -1)
    extrap = face_extrap.T
    wall_lift = wall_lift.T
    tall = prism_state.shape[1]
    side = pltpu.VMEM((FP, capacity), BF)
    hbm = pltpu.with_memory_space_constraint
    operands = (burn, owner, prism_state, wall_extrap, tet_state, code, extrap)
    part, owned, prism, wall, tet, code, extrap = call(
        wall_kernel,
        "walls",
        (pltpu.VMEM((8, 128), F32), pltpu.VMEM((8, tall), F32)) + tuple(like(x) for x in operands[2:]),
        (VM,) * 7,
        [HB] * 7,
        5_000_000_000,
        3_000_000,
        tuple(hbm(x, pltpu.HBM) for x in operands),
        [like(x) for x in operands[:2]] + [pltpu.SemaphoreType.DMA((7,))],
    )
    odd, even = call(
        face_kernel, "faces", (side, side), (VM, VM), [VM] * 3, 5_000_000_000, 600_000, (code, tet, extrap)
    )
    part, tet_volume, prism_volume, face_lift, wall_lift, law, face_count, area = lax.optimization_barrier(
        (part, tet_volume, prism_volume, face_lift, wall_lift, burn_law, face_count, area)
    )
    half = swap(part, "azim", ((0, 3), (1, 2)))
    count = lax.axis_size("axial")
    from_even = swap(even, "axial", [(i, i + 1) for i in range(0, count - 1, 2)])
    from_odd = swap(odd, "axial", [(i, i + 1) for i in range(1, count - 1, 2)])
    pair = part + half
    other = swap(pair, "azim", ((0, 1), (2, 3)))
    pair, tet, prism = lax.optimization_barrier((pair, tet, prism))
    tet_part, prism_part, rows, gain, pad, live = call(
        local_kernel,
        "local",
        (
            pltpu.VMEM(tet.shape, F32),
            pltpu.VMEM(prism.shape, F32),
            pltpu.VMEM((FW, tall), F32),
            pltpu.VMEM((FW, tall), F32),
            pltpu.VMEM((tet.shape[0], 4 * FP), BF),
            like(area),
        ),
        (VM,) * 6,
        [VM] * 10,
        5_000_000_000,
        4_000_000,
        (tet, prism, wall, owned, tet_volume, prism_volume, face_lift, law, face_count, area),
    )
    tet_new = call(
        tet_kernel,
        "tet_finish",
        like(tet),
        VM,
        [VM] * 8,
        5_000_000_000,
        3_000_000,
        (code, live, odd, even, from_odd, from_even, tet_part, pad),
    )
    tet_new, prism_new = call(
        prism_kernel,
        "prism_finish",
        (jax.ShapeDtypeStruct(tet.shape, BF), jax.ShapeDtypeStruct(prism.shape, BF)),
        (HB, HB),
        [VM] * 9,
        5_000_000_000,
        3_000_000,
        (tet_new, pair, other, law, owned, rows, gain, prism_part, wall_lift),
        [like(prism), pltpu.SemaphoreType.DMA((5,))],
    )
    return (tet_new, prism_new)


def solution(mesh):
    elements = P(None, ("axial", "azim"))
    placed = (
        elements,
        elements,
        P(),
        P(),
        P(),
        P(),
        P(),
        P(),
        P(("axial", "azim")),
        P(("axial", "azim"), None),
        P(("axial", "azim")),
        P(("axial", "azim")),
        P(("axial", "azim"), None),
        P("axial", None, None),
    )
    return jax.shard_map(
        on_device, mesh=mesh, in_specs=placed, out_specs=(elements, elements), check_vma=False
    )
```

```python
import jax
import jax.numpy as jnp
from jax import lax
from jax.experimental import pallas as pl
from jax.experimental.pallas import tpu as pltpu
from jax.sharding import PartitionSpec as P

NV = 5
TFP = 15
FW = 75
FP = 80
BW_DEV = 512
SECTORS = 4
STEP = 0.25

BF = jnp.bfloat16
F32 = jnp.float32
NN = (((1,), (0,)), ((), ()))
NT = (((1,), (1,)), ((), ()))
TN = (((0,), (0,)), ((), ()))


def mm(a, b, dims=NN):
    return lax.dot_general(a, b, dims, preferred_element_type=F32)


def rows_of(shape):
    return lax.broadcasted_iota(jnp.int32, shape, 0)


def cols_of(shape):
    return lax.broadcasted_iota(jnp.int32, shape, 1)


def hot(mask):
    return jnp.where(mask, 1.0, 0.0).astype(BF)


def spread(rows, cols):
    r = rows_of((rows, cols))
    f = (r >= FP).astype(jnp.int32) + (r >= 2 * FP).astype(jnp.int32) + (r >= 3 * FP).astype(jnp.int32)
    c = cols_of((rows, cols))
    return hot((c == r - (FP - FW) * f) & (r - FP * f < FW))


def square_half(values):
    wide = values.astype(F32)
    return (0.5 * wide * wide).astype(BF)


def faces_of(code, state, pad):
    pick = hot(rows_of((state.shape[1], code.shape[1])) == (code >> 2))
    wide = mm(pad, mm(state, pick).astype(BF))
    face = code & 3
    return jnp.where(
        face < 2,
        jnp.where(face == 0, wide[:FP], wide[FP : 2 * FP]),
        jnp.where(face == 2, wide[2 * FP : 3 * FP], wide[3 * FP :]),
    ).astype(BF)


def first_side():
    return 1 - (lax.axis_index("axial") & 1)


def side_of(ref, side):
    width = ref.shape[1] // 2
    return ref[:, pl.ds(pl.multiple_of(side * width, width), width)]


def wall_kernel(
    burn_hbm, owner_hbm, prism_hbm, wall_hbm, tet_hbm, code_hbm, extrap_hbm,
    part_ref, owned_ref, prism_ref, wall_ref, tet_ref, code_ref, extrap_ref,
    burn_ref, owner_ref, sems,
):
    pairs = (
        (burn_hbm, burn_ref), (owner_hbm, owner_ref), (prism_hbm, prism_ref), (wall_hbm, wall_ref),
        (tet_hbm, tet_ref), (code_hbm, code_ref), (extrap_hbm, extrap_ref),
    )
    copies = [pltpu.make_async_copy(a, b, sems.at[n]) for n, (a, b) in enumerate(pairs)]
    for copy in copies:
        copy.start()
    for copy in copies[:2]:
        copy.wait()
    walls = burn_ref.shape[1]
    place = hot(rows_of((prism_ref.shape[1], walls)) == burn_ref[...])
    owned = mm(hot(rows_of((8, walls)) == owner_ref[...]), place, NT)
    owned_ref[...] = owned
    for copy in copies[2:4]:
        copy.wait()
    rows = mm(wall_ref[(NV - 1) * TFP : NV * TFP, :], prism_ref[...]).astype(BF).astype(F32)
    sums = jnp.sum(rows * rows, axis=0, keepdims=True)
    part_ref[...] = jnp.broadcast_to(jnp.sum(owned * sums, axis=1, keepdims=True), part_ref.shape)
    for copy in copies[4:]:
        copy.wait()


def early():
    axial = lax.axis_index("axial")
    return (axial < 2) & (axial + lax.axis_index("azim") > 0)


def make_faces(code_ref, tet_ref, extrap_ref, odd_ref, even_ref):
    capacity = odd_ref.shape[1]
    pad = mm(spread(4 * FP, 4 * FW), extrap_ref[...], NT).astype(BF)
    left = faces_of(code_ref[...], tet_ref[...], pad)
    upper = first_side() == 1
    odd_ref[...] = jnp.where(upper, left[:, :capacity], left[:, capacity:])
    even_ref[...] = jnp.where(upper, left[:, capacity:], left[:, :capacity])


def make_local(
    tet_ref, prism_ref, wall_ref, owned_ref, volume_ref, prism_volume_ref, lift_ref, law_ref, count_ref, area_ref,
    tet_part_ref, prism_part_ref, rows_ref, gain_ref, pad_ref, live_ref,
):
    rows = mm(wall_ref[...], prism_ref[...]).astype(BF).astype(F32)
    elements = rows.shape[1]
    any_owner = jnp.sum(owned_ref[:SECTORS, :], axis=0, keepdims=True)
    rows_ref[...] = jnp.where(any_owner > 0.5, rows, 0.0)
    pressure = rows[(NV - 1) * TFP :]
    squares = jnp.concatenate([pressure * pressure] * NV, axis=0)
    v = rows_of((FW, 128)) // TFP
    weight = jnp.zeros((FW, elements), F32)
    for o in range(SECTORS):
        column = jnp.zeros((FW, 128), F32)
        for k in range(NV):
            gain = law_ref[0, o : o + 1, 1 + k : 2 + k] * law_ref[0, o : o + 1, 0:1]
            column = jnp.where(v == k, gain, column)
        column = jnp.concatenate([column] * (elements // 128), axis=1)
        weight = jnp.where(owned_ref[o : o + 1, :] > 0.5, column, weight)
    gain_ref[...] = weight * squares
    state = prism_ref[...]
    prism_part_ref[...] = state.astype(F32) - STEP * mm(prism_volume_ref[...], square_half(state))
    state = tet_ref[...]
    tet_part_ref[...] = state.astype(F32) - STEP * mm(volume_ref[...], square_half(state))
    pad_ref[...] = mm(lift_ref[...], spread(4 * FP, 4 * FW), NT).astype(BF)
    capacity = live_ref.shape[1] // 2
    slot = cols_of((1, capacity))
    for side in range(2):
        area = area_ref[:, side * capacity : (side + 1) * capacity]
        live_ref[:, side * capacity : (side + 1) * capacity] = jnp.where(slot < count_ref[:, side : side + 1], area, 0.0)


def early_kernel(
    code_ref, extrap_ref, tet_ref, prism_ref, wall_ref, owned_ref,
    volume_hbm, prism_volume_hbm, lift_hbm, law_hbm, count_hbm, area_hbm,
    odd_ref, even_ref, tet_part_ref, prism_part_ref, rows_ref, gain_ref, pad_ref, live_ref,
    volume_ref, prism_volume_ref, lift_ref, law_ref, count_ref, area_ref, sems,
):
    @pl.when(early())
    def _():
        pairs = (
            (volume_hbm, volume_ref), (prism_volume_hbm, prism_volume_ref), (lift_hbm, lift_ref),
            (law_hbm, law_ref), (count_hbm, count_ref), (area_hbm, area_ref),
        )
        copies = [pltpu.make_async_copy(a, b, sems.at[n]) for n, (a, b) in enumerate(pairs)]
        for copy in copies:
            copy.start()
        make_faces(code_ref, tet_ref, extrap_ref, odd_ref, even_ref)
        for copy in copies:
            copy.wait()
        make_local(
            tet_ref, prism_ref, wall_ref, owned_ref, volume_ref, prism_volume_ref, lift_ref, law_ref, count_ref, area_ref,
            tet_part_ref, prism_part_ref, rows_ref, gain_ref, pad_ref, live_ref,
        )


def face_kernel(code_ref, tet_ref, extrap_ref, odd_in, even_in, odd_ref, even_ref):
    @pl.when(jnp.logical_not(early()))
    def _():
        make_faces(code_ref, tet_ref, extrap_ref, odd_ref, even_ref)


def local_kernel(
    tet_ref, prism_ref, wall_ref, owned_ref, volume_ref, prism_volume_ref, lift_ref, law_ref, count_ref, area_ref,
    tet_part_in, prism_part_in, rows_in, gain_in, pad_in, live_in,
    tet_part_ref, prism_part_ref, rows_ref, gain_ref, pad_ref, live_ref,
):
    @pl.when(jnp.logical_not(early()))
    def _():
        make_local(
            tet_ref, prism_ref, wall_ref, owned_ref, volume_ref, prism_volume_ref, lift_ref, law_ref, count_ref, area_ref,
            tet_part_ref, prism_part_ref, rows_ref, gain_ref, pad_ref, live_ref,
        )


def tet_kernel(code_ref, live_ref, odd_ref, even_ref, from_odd_ref, from_even_ref, part_ref, pad_ref, out_ref):
    first = first_side()
    capacity = even_ref.shape[1]
    elements = part_ref.shape[1]
    placed = None
    for side, own, other in ((1 - first, odd_ref, from_odd_ref), (first, even_ref, from_even_ref)):
        code = side_of(code_ref, side)
        live = side_of(live_ref, side)
        normal = jnp.where(side == 0, -0.25, 0.25)
        left = own[...].astype(F32)
        right = other[...].astype(F32)
        speed = jnp.maximum(jnp.abs(left), jnp.abs(right))
        flux = normal * (right * right - left * left) - 0.5 * speed * (right - left)
        jump = (live * flux).astype(BF)
        face = code & 3
        masked = jnp.concatenate([jnp.where(face == f, jump, jnp.zeros_like(jump)) for f in range(4)], axis=0)
        pick = hot(rows_of((elements, capacity)) == (code >> 2))
        piece = mm(masked, pick, NT)
        placed = piece if placed is None else placed + piece
    out_ref[...] = (part_ref[...] - STEP * mm(pad_ref[...], placed.astype(BF))).astype(BF)


def prism_kernel(
    tet_ref, pair_ref, other_ref, law_ref, owned_ref, rows_ref, gain_ref, part_ref, lift_ref,
    tet_hbm, prism_hbm, prism_ref, sems,
):
    tet_out = pltpu.make_async_copy(tet_ref, tet_hbm, sems.at[0])
    tet_out.start()
    sums = (pair_ref[...] + other_ref[...])[:SECTORS]
    damping = 1.0 / (1.0 + law_ref[0, :, 0:1] * sums / (BW_DEV * TFP))
    elements = part_ref.shape[1]
    width = elements // 4
    lift = lift_ref[...]
    outs = []
    for n in range(4):
        at = slice(n * width, (n + 1) * width)
        factor = jnp.zeros((1, width), F32)
        for o in range(SECTORS):
            row = jnp.concatenate([damping[o : o + 1]] * (width // 128), axis=1)
            factor = jnp.where(owned_ref[o : o + 1, at] > 0.5, row, factor)
        jump = (gain_ref[:, at] * factor - rows_ref[:, at]).astype(BF)
        prism_ref[:, at] = (part_ref[:, at] - STEP * mm(lift, jump, TN)).astype(BF)
        out = pltpu.make_async_copy(prism_ref.at[:, at], prism_hbm.at[:, at], sems.at[1 + n])
        out.start()
        outs.append(out)
    for out in outs:
        out.wait()
    tet_out.wait()


VM = pl.BlockSpec(memory_space=pltpu.VMEM)
HB = pl.BlockSpec(memory_space=pltpu.HBM)


def call(kernel, name, outs, out_specs, specs, flops, moved, args, scratch=(), aliases=()):
    return pl.pallas_call(
        kernel,
        out_shape=outs,
        in_specs=specs,
        out_specs=out_specs,
        scratch_shapes=scratch,
        input_output_aliases=dict(aliases),
        cost_estimate=pl.CostEstimate(flops=flops, bytes_accessed=moved, transcendentals=0),
        compiler_params=pltpu.CompilerParams(vmem_limit_bytes=32 * 1024 * 1024),
        name=name,
    )(*args)


def like(value):
    return pltpu.VMEM(value.shape, value.dtype)


def swap(value, axis, pairs):
    return lax.ppermute(value, axis, list(pairs) + [(j, i) for i, j in pairs])


def on_device(
    tet_state,
    prism_state,
    tet_volume,
    prism_volume,
    face_extrap,
    face_lift,
    wall_extrap,
    wall_lift,
    face_code,
    face_count,
    face_area,
    burn_prism,
    burn_owner,
    burn_law,
):
    slots = face_code.shape[0]
    capacity = slots // 2
    code = face_code.reshape(1, slots)
    area = face_area.reshape(1, slots)
    burn = burn_prism.reshape(1, -1)
    owner = burn_owner.reshape(1, -1)
    extrap = face_extrap.T
    wall_lift = wall_lift.T
    tall = prism_state.shape[1]
    side = pltpu.VMEM((FP, capacity), BF)
    hbm = pltpu.with_memory_space_constraint
    operands = (burn, owner, prism_state, wall_extrap, tet_state, code, extrap)
    part, owned, prism, wall, tet, code, extrap = call(
        wall_kernel,
        "walls",
        (pltpu.VMEM((8, 128), F32), pltpu.VMEM((8, tall), F32)) + tuple(like(x) for x in operands[2:]),
        (VM,) * 7,
        [HB] * 7,
        5_000_000_000,
        3_000_000,
        tuple(hbm(x, pltpu.HBM) for x in operands),
        [like(x) for x in operands[:2]] + [pltpu.SemaphoreType.DMA((7,))],
    )
    local_outs = (
        pltpu.VMEM(tet.shape, F32),
        pltpu.VMEM(prism.shape, F32),
        pltpu.VMEM((FW, tall), F32),
        pltpu.VMEM((FW, tall), F32),
        pltpu.VMEM((tet.shape[0], 4 * FP), BF),
        like(area),
    )
    operands = (tet_volume, prism_volume, face_lift, burn_law, face_count, area)
    odd, even, *made = call(
        early_kernel,
        "early",
        (side, side) + local_outs,
        (VM,) * 8,
        [VM] * 6 + [HB] * 6,
        5_000_000_000,
        3_000_000,
        (code, extrap, tet, prism, wall, owned) + tuple(hbm(x, pltpu.HBM) for x in operands),
        [like(x) for x in operands] + [pltpu.SemaphoreType.DMA((6,))],
    )
    part, odd, even, *made = lax.optimization_barrier((part, odd, even, *made))
    odd, even = call(
        face_kernel, "faces", (side, side), (VM, VM), [VM] * 5, 5_000_000_000, 600_000, (code, tet, extrap, odd, even),
        aliases=((3, 0), (4, 1)),
    )
    part, tet_volume, prism_volume, face_lift, wall_lift, law, face_count, area = lax.optimization_barrier(
        (part, tet_volume, prism_volume, face_lift, wall_lift, burn_law, face_count, area)
    )
    half = swap(part, "azim", ((0, 3), (1, 2)))
    count = lax.axis_size("axial")
    from_even = swap(even, "axial", [(i, i + 1) for i in range(0, count - 1, 2)])
    from_odd = swap(odd, "axial", [(i, i + 1) for i in range(1, count - 1, 2)])
    pair = part + half
    other = swap(pair, "azim", ((0, 1), (2, 3)))
    pair, tet, prism = lax.optimization_barrier((pair, tet, prism))
    tet_part, prism_part, rows, gain, pad, live = call(
        local_kernel,
        "local",
        local_outs,
        (VM,) * 6,
        [VM] * 16,
        5_000_000_000,
        4_000_000,
        (tet, prism, wall, owned, tet_volume, prism_volume, face_lift, law, face_count, area, *made),
        aliases=tuple((10 + n, n) for n in range(6)),
    )
    tet_new = call(
        tet_kernel,
        "tet_finish",
        like(tet),
        VM,
        [VM] * 8,
        5_000_000_000,
        3_000_000,
        (code, live, odd, even, from_odd, from_even, tet_part, pad),
    )
    tet_new, prism_new = call(
        prism_kernel,
        "prism_finish",
        (jax.ShapeDtypeStruct(tet.shape, BF), jax.ShapeDtypeStruct(prism.shape, BF)),
        (HB, HB),
        [VM] * 9,
        5_000_000_000,
        3_000_000,
        (tet_new, pair, other, law, owned, rows, gain, prism_part, wall_lift),
        [like(prism), pltpu.SemaphoreType.DMA((5,))],
    )
    return (tet_new, prism_new)


def solution(mesh):
    elements = P(None, ("axial", "azim"))
    placed = (
        elements,
        elements,
        P(),
        P(),
        P(),
        P(),
        P(),
        P(),
        P(("axial", "azim")),
        P(("axial", "azim"), None),
        P(("axial", "azim")),
        P(("axial", "azim")),
        P(("axial", "azim"), None),
        P("axial", None, None),
    )
    return jax.shard_map(
        on_device, mesh=mesh, in_specs=placed, out_specs=(elements, elements), check_vma=False
    )
```

```python
import jax
import jax.numpy as jnp
from jax import lax
from jax.experimental import pallas as pl
from jax.experimental.pallas import tpu as pltpu
from jax.sharding import PartitionSpec as P

NV = 5
TFP = 15
FW = 75
FP = 80
BW_DEV = 512
SECTORS = 4
STEP = 0.25

BF = jnp.bfloat16
F32 = jnp.float32
NN = (((1,), (0,)), ((), ()))
NT = (((1,), (1,)), ((), ()))
TN = (((0,), (0,)), ((), ()))


def mm(a, b, dims=NN):
    return lax.dot_general(a, b, dims, preferred_element_type=F32)


def rows_of(shape):
    return lax.broadcasted_iota(jnp.int32, shape, 0)


def cols_of(shape):
    return lax.broadcasted_iota(jnp.int32, shape, 1)


def hot(mask):
    return jnp.where(mask, 1.0, 0.0).astype(BF)


def spread(rows, cols):
    r = rows_of((rows, cols))
    f = (r >= FP).astype(jnp.int32) + (r >= 2 * FP).astype(jnp.int32) + (r >= 3 * FP).astype(jnp.int32)
    c = cols_of((rows, cols))
    return hot((c == r - (FP - FW) * f) & (r - FP * f < FW))


def square_half(values):
    wide = values.astype(F32)
    return (0.5 * wide * wide).astype(BF)


def faces_of(code, state, pad):
    pick = hot(rows_of((state.shape[1], code.shape[1])) == (code >> 2))
    wide = mm(pad, mm(state, pick).astype(BF))
    face = code & 3
    return jnp.where(
        face < 2,
        jnp.where(face == 0, wide[:FP], wide[FP : 2 * FP]),
        jnp.where(face == 2, wide[2 * FP : 3 * FP], wide[3 * FP :]),
    ).astype(BF)


def first_side():
    return 1 - (lax.axis_index("axial") & 1)


def side_of(ref, side):
    width = ref.shape[1] // 2
    return ref[:, pl.ds(pl.multiple_of(side * width, width), width)]


def early():
    axial = lax.axis_index("axial")
    return (axial < 2) & (axial + lax.axis_index("azim") > 0)


def make_faces(code_ref, tet_ref, extrap_ref, odd_ref, even_ref):
    capacity = odd_ref.shape[1]
    pad = mm(spread(4 * FP, 4 * FW), extrap_ref[...], NT).astype(BF)
    left = faces_of(code_ref[...], tet_ref[...], pad)
    upper = first_side() == 1
    odd_ref[...] = jnp.where(upper, left[:, :capacity], left[:, capacity:])
    even_ref[...] = jnp.where(upper, left[:, capacity:], left[:, :capacity])


def make_local(
    tet_ref, prism_ref, wall_ref, owned_ref, volume_ref, prism_volume_ref, lift_ref, law_ref, count_ref, area_ref,
    tet_part_ref, prism_part_ref, rows_ref, gain_ref, pad_ref, live_ref,
):
    rows = mm(wall_ref[...], prism_ref[...]).astype(BF).astype(F32)
    elements = rows.shape[1]
    any_owner = jnp.sum(owned_ref[:SECTORS, :], axis=0, keepdims=True)
    rows_ref[...] = jnp.where(any_owner > 0.5, rows, 0.0)
    pressure = rows[(NV - 1) * TFP :]
    squares = jnp.concatenate([pressure * pressure] * NV, axis=0)
    v = rows_of((FW, 128)) // TFP
    weight = jnp.zeros((FW, elements), F32)
    for o in range(SECTORS):
        column = jnp.zeros((FW, 128), F32)
        for k in range(NV):
            gain = law_ref[0, o : o + 1, 1 + k : 2 + k] * law_ref[0, o : o + 1, 0:1]
            column = jnp.where(v == k, gain, column)
        column = jnp.concatenate([column] * (elements // 128), axis=1)
        weight = jnp.where(owned_ref[o : o + 1, :] > 0.5, column, weight)
    gain_ref[...] = weight * squares
    state = prism_ref[...]
    prism_part_ref[...] = state.astype(F32) - STEP * mm(prism_volume_ref[...], square_half(state))
    state = tet_ref[...]
    tet_part_ref[...] = state.astype(F32) - STEP * mm(volume_ref[...], square_half(state))
    pad_ref[...] = mm(lift_ref[...], spread(4 * FP, 4 * FW), NT).astype(BF)
    capacity = live_ref.shape[1] // 2
    slot = cols_of((1, capacity))
    for side in range(2):
        area = area_ref[:, side * capacity : (side + 1) * capacity]
        live_ref[:, side * capacity : (side + 1) * capacity] = jnp.where(slot < count_ref[:, side : side + 1], area, 0.0)


def wall_kernel(
    burn_hbm, owner_hbm, prism_hbm, wall_hbm, tet_hbm, code_hbm, extrap_hbm,
    volume_hbm, prism_volume_hbm, lift_hbm, law_hbm, count_hbm, area_hbm,
    part_ref, owned_ref, prism_ref, wall_ref, tet_ref, code_ref, extrap_ref,
    odd_ref, even_ref, tet_part_ref, prism_part_ref, rows_ref, gain_ref, pad_ref, live_ref,
    burn_ref, owner_ref, volume_ref, prism_volume_ref, lift_ref, law_ref, count_ref, area_ref, sems,
):
    pairs = (
        (burn_hbm, burn_ref), (owner_hbm, owner_ref), (prism_hbm, prism_ref), (wall_hbm, wall_ref),
        (tet_hbm, tet_ref), (code_hbm, code_ref), (extrap_hbm, extrap_ref),
    )
    copies = [pltpu.make_async_copy(a, b, sems.at[n]) for n, (a, b) in enumerate(pairs)]
    for copy in copies:
        copy.start()
    for copy in copies[:2]:
        copy.wait()
    walls = burn_ref.shape[1]
    place = hot(rows_of((prism_ref.shape[1], walls)) == burn_ref[...])
    owned = mm(hot(rows_of((8, walls)) == owner_ref[...]), place, NT)
    owned_ref[...] = owned
    for copy in copies[2:4]:
        copy.wait()
    rows = mm(wall_ref[(NV - 1) * TFP : NV * TFP, :], prism_ref[...]).astype(BF).astype(F32)
    sums = jnp.sum(rows * rows, axis=0, keepdims=True)
    part_ref[...] = jnp.broadcast_to(jnp.sum(owned * sums, axis=1, keepdims=True), part_ref.shape)
    for copy in copies[4:]:
        copy.wait()

    @pl.when(early())
    def _():
        more = (
            (volume_hbm, volume_ref), (prism_volume_hbm, prism_volume_ref), (lift_hbm, lift_ref),
            (law_hbm, law_ref), (count_hbm, count_ref), (area_hbm, area_ref),
        )
        late = [pltpu.make_async_copy(a, b, sems.at[len(pairs) + n]) for n, (a, b) in enumerate(more)]
        for copy in late:
            copy.start()
        make_faces(code_ref, tet_ref, extrap_ref, odd_ref, even_ref)
        for copy in late:
            copy.wait()
        make_local(
            tet_ref, prism_ref, wall_ref, owned_ref, volume_ref, prism_volume_ref, lift_ref, law_ref, count_ref, area_ref,
            tet_part_ref, prism_part_ref, rows_ref, gain_ref, pad_ref, live_ref,
        )


def face_kernel(code_ref, tet_ref, extrap_ref, odd_in, even_in, odd_ref, even_ref):
    axial = lax.axis_index("axial")

    @pl.when(jnp.logical_not(early()) & (axial > 0))
    def _():
        make_faces(code_ref, tet_ref, extrap_ref, odd_ref, even_ref)

    @pl.when(jnp.logical_not(early()) & (axial == 0))
    def _():
        capacity = odd_ref.shape[1]
        pad = mm(spread(4 * FP, 4 * FW), extrap_ref[...], NT).astype(BF)
        odd_ref[...] = jnp.zeros_like(odd_ref)
        even_ref[...] = faces_of(code_ref[:, capacity:], tet_ref[...], pad)


def local_kernel(
    tet_ref, prism_ref, wall_ref, owned_ref, volume_ref, prism_volume_ref, lift_ref, law_ref, count_ref, area_ref,
    tet_part_in, prism_part_in, rows_in, gain_in, pad_in, live_in,
    tet_part_ref, prism_part_ref, rows_ref, gain_ref, pad_ref, live_ref,
):
    @pl.when(jnp.logical_not(early()))
    def _():
        make_local(
            tet_ref, prism_ref, wall_ref, owned_ref, volume_ref, prism_volume_ref, lift_ref, law_ref, count_ref, area_ref,
            tet_part_ref, prism_part_ref, rows_ref, gain_ref, pad_ref, live_ref,
        )


def tet_kernel(code_ref, live_ref, odd_ref, even_ref, from_odd_ref, from_even_ref, part_ref, pad_ref, out_ref):
    first = first_side()
    capacity = even_ref.shape[1]
    elements = part_ref.shape[1]
    placed = None
    for side, own, other in ((1 - first, odd_ref, from_odd_ref), (first, even_ref, from_even_ref)):
        code = side_of(code_ref, side)
        live = side_of(live_ref, side)
        normal = jnp.where(side == 0, -0.25, 0.25)
        left = own[...].astype(F32)
        right = other[...].astype(F32)
        speed = jnp.maximum(jnp.abs(left), jnp.abs(right))
        flux = normal * (right * right - left * left) - 0.5 * speed * (right - left)
        jump = (live * flux).astype(BF)
        face = code & 3
        masked = jnp.concatenate([jnp.where(face == f, jump, jnp.zeros_like(jump)) for f in range(4)], axis=0)
        pick = hot(rows_of((elements, capacity)) == (code >> 2))
        piece = mm(masked, pick, NT)
        placed = piece if placed is None else placed + piece
    out_ref[...] = (part_ref[...] - STEP * mm(pad_ref[...], placed.astype(BF))).astype(BF)


def prism_kernel(
    tet_ref, pair_ref, other_ref, law_ref, owned_ref, rows_ref, gain_ref, part_ref, lift_ref,
    tet_hbm, prism_hbm, prism_ref, sems,
):
    tet_out = pltpu.make_async_copy(tet_ref, tet_hbm, sems.at[0])
    tet_out.start()
    sums = (pair_ref[...] + other_ref[...])[:SECTORS]
    damping = 1.0 / (1.0 + law_ref[0, :, 0:1] * sums / (BW_DEV * TFP))
    elements = part_ref.shape[1]
    width = elements // 4
    lift = lift_ref[...]
    outs = []
    for n in range(4):
        at = slice(n * width, (n + 1) * width)
        factor = jnp.zeros((1, width), F32)
        for o in range(SECTORS):
            row = jnp.concatenate([damping[o : o + 1]] * (width // 128), axis=1)
            factor = jnp.where(owned_ref[o : o + 1, at] > 0.5, row, factor)
        jump = (gain_ref[:, at] * factor - rows_ref[:, at]).astype(BF)
        prism_ref[:, at] = (part_ref[:, at] - STEP * mm(lift, jump, TN)).astype(BF)
        out = pltpu.make_async_copy(prism_ref.at[:, at], prism_hbm.at[:, at], sems.at[1 + n])
        out.start()
        outs.append(out)
    for out in outs:
        out.wait()
    tet_out.wait()


VM = pl.BlockSpec(memory_space=pltpu.VMEM)
HB = pl.BlockSpec(memory_space=pltpu.HBM)


def call(kernel, name, outs, out_specs, specs, flops, moved, args, scratch=(), aliases=()):
    return pl.pallas_call(
        kernel,
        out_shape=outs,
        in_specs=specs,
        out_specs=out_specs,
        scratch_shapes=scratch,
        input_output_aliases=dict(aliases),
        cost_estimate=pl.CostEstimate(flops=flops, bytes_accessed=moved, transcendentals=0),
        compiler_params=pltpu.CompilerParams(vmem_limit_bytes=32 * 1024 * 1024),
        name=name,
    )(*args)


def like(value):
    return pltpu.VMEM(value.shape, value.dtype)


def swap(value, axis, pairs):
    return lax.ppermute(value, axis, list(pairs) + [(j, i) for i, j in pairs])


def on_device(
    tet_state,
    prism_state,
    tet_volume,
    prism_volume,
    face_extrap,
    face_lift,
    wall_extrap,
    wall_lift,
    face_code,
    face_count,
    face_area,
    burn_prism,
    burn_owner,
    burn_law,
):
    slots = face_code.shape[0]
    capacity = slots // 2
    code = face_code.reshape(1, slots)
    area = face_area.reshape(1, slots)
    burn = burn_prism.reshape(1, -1)
    owner = burn_owner.reshape(1, -1)
    extrap = face_extrap.T
    wall_lift = wall_lift.T
    tall = prism_state.shape[1]
    side = pltpu.VMEM((FP, capacity), BF)
    hbm = pltpu.with_memory_space_constraint
    operands = (burn, owner, prism_state, wall_extrap, tet_state, code, extrap)
    more = (tet_volume, prism_volume, face_lift, burn_law, face_count, area)
    local_outs = (
        pltpu.VMEM(tet_state.shape, F32),
        pltpu.VMEM(prism_state.shape, F32),
        pltpu.VMEM((FW, tall), F32),
        pltpu.VMEM((FW, tall), F32),
        pltpu.VMEM((tet_state.shape[0], 4 * FP), BF),
        like(area),
    )
    part, owned, prism, wall, tet, code, extrap, odd, even, *made = call(
        wall_kernel,
        "walls",
        (pltpu.VMEM((8, 128), F32), pltpu.VMEM((8, tall), F32))
        + tuple(like(x) for x in operands[2:])
        + (side, side)
        + local_outs,
        (VM,) * 15,
        [HB] * 13,
        5_000_000_000,
        3_000_000,
        tuple(hbm(x, pltpu.HBM) for x in operands + more),
        [like(x) for x in operands[:2] + more] + [pltpu.SemaphoreType.DMA((13,))],
    )
    odd, even = call(
        face_kernel, "faces", (side, side), (VM, VM), [VM] * 5, 5_000_000_000, 600_000, (code, tet, extrap, odd, even),
        aliases=((3, 0), (4, 1)),
    )
    part, tet_volume, prism_volume, face_lift, wall_lift, law, face_count, area = lax.optimization_barrier(
        (part, tet_volume, prism_volume, face_lift, wall_lift, burn_law, face_count, area)
    )
    half = swap(part, "azim", ((0, 3), (1, 2)))
    count = lax.axis_size("axial")
    from_even = swap(even, "axial", [(i, i + 1) for i in range(0, count - 1, 2)])
    from_odd = swap(odd, "axial", [(i, i + 1) for i in range(1, count - 1, 2)])
    pair = part + half
    other = swap(pair, "azim", ((0, 1), (2, 3)))
    pair, tet, prism = lax.optimization_barrier((pair, tet, prism))
    tet_part, prism_part, rows, gain, pad, live = call(
        local_kernel,
        "local",
        local_outs,
        (VM,) * 6,
        [VM] * 16,
        5_000_000_000,
        4_000_000,
        (tet, prism, wall, owned, tet_volume, prism_volume, face_lift, law, face_count, area, *made),
        aliases=tuple((10 + n, n) for n in range(6)),
    )
    tet_new = call(
        tet_kernel,
        "tet_finish",
        like(tet),
        VM,
        [VM] * 8,
        5_000_000_000,
        3_000_000,
        (code, live, odd, even, from_odd, from_even, tet_part, pad),
    )
    tet_new, prism_new = call(
        prism_kernel,
        "prism_finish",
        (jax.ShapeDtypeStruct(tet.shape, BF), jax.ShapeDtypeStruct(prism.shape, BF)),
        (HB, HB),
        [VM] * 9,
        5_000_000_000,
        3_000_000,
        (tet_new, pair, other, law, owned, rows, gain, prism_part, wall_lift),
        [like(prism), pltpu.SemaphoreType.DMA((5,))],
    )
    return (tet_new, prism_new)


def solution(mesh):
    elements = P(None, ("axial", "azim"))
    placed = (
        elements,
        elements,
        P(),
        P(),
        P(),
        P(),
        P(),
        P(),
        P(("axial", "azim")),
        P(("axial", "azim"), None),
        P(("axial", "azim")),
        P(("axial", "azim")),
        P(("axial", "azim"), None),
        P("axial", None, None),
    )
    return jax.shard_map(
        on_device, mesh=mesh, in_specs=placed, out_specs=(elements, elements), check_vma=False
    )
```

```python
import jax
import jax.numpy as jnp
from jax import lax
from jax.experimental import pallas as pl
from jax.experimental.pallas import tpu as pltpu
from jax.sharding import PartitionSpec as P

NV = 5
TFP = 15
FW = 75
FP = 80
BW_DEV = 512
SECTORS = 4
STEP = 0.25

BF = jnp.bfloat16
F32 = jnp.float32
NN = (((1,), (0,)), ((), ()))
NT = (((1,), (1,)), ((), ()))
TN = (((0,), (0,)), ((), ()))


def mm(a, b, dims=NN):
    return lax.dot_general(a, b, dims, preferred_element_type=F32)


def rows_of(shape):
    return lax.broadcasted_iota(jnp.int32, shape, 0)


def cols_of(shape):
    return lax.broadcasted_iota(jnp.int32, shape, 1)


def hot(mask):
    return jnp.where(mask, 1.0, 0.0).astype(BF)


def spread(rows, cols):
    r = rows_of((rows, cols))
    f = (r >= FP).astype(jnp.int32) + (r >= 2 * FP).astype(jnp.int32) + (r >= 3 * FP).astype(jnp.int32)
    c = cols_of((rows, cols))
    return hot((c == r - (FP - FW) * f) & (r - FP * f < FW))


def square_half(values):
    wide = values.astype(F32)
    return (0.5 * wide * wide).astype(BF)


def faces_of(code, state, pad):
    pick = hot(rows_of((state.shape[1], code.shape[1])) == (code >> 2))
    wide = mm(pad, mm(state, pick).astype(BF))
    face = code & 3
    return jnp.where(
        face < 2,
        jnp.where(face == 0, wide[:FP], wide[FP : 2 * FP]),
        jnp.where(face == 2, wide[2 * FP : 3 * FP], wide[3 * FP :]),
    ).astype(BF)


def first_side():
    return 1 - (lax.axis_index("axial") & 1)


def side_of(ref, side):
    width = ref.shape[1] // 2
    return ref[:, pl.ds(pl.multiple_of(side * width, width), width)]


def early():
    axial = lax.axis_index("axial")
    return (axial < 2) & (axial + lax.axis_index("azim") > 0)


def make_faces(code_ref, tet_ref, extrap_ref, odd_ref, even_ref):
    capacity = odd_ref.shape[1]
    pad = mm(spread(4 * FP, 4 * FW), extrap_ref[...], NT).astype(BF)
    left = faces_of(code_ref[...], tet_ref[...], pad)
    upper = first_side() == 1
    odd_ref[...] = jnp.where(upper, left[:, :capacity], left[:, capacity:])
    even_ref[...] = jnp.where(upper, left[:, capacity:], left[:, :capacity])


def make_local(
    tet_ref, prism_ref, wall_ref, owned_ref, volume_ref, prism_volume_ref, lift_ref, law_ref, count_ref, area_ref,
    tet_part_ref, prism_part_ref, rows_ref, gain_ref, pad_ref, live_ref,
):
    rows = mm(wall_ref[...], prism_ref[...]).astype(BF).astype(F32)
    elements = rows.shape[1]
    any_owner = jnp.sum(owned_ref[:SECTORS, :], axis=0, keepdims=True)
    rows_ref[...] = jnp.where(any_owner > 0.5, rows, 0.0)
    pressure = rows[(NV - 1) * TFP :]
    squares = jnp.concatenate([pressure * pressure] * NV, axis=0)
    v = rows_of((FW, 128)) // TFP
    weight = jnp.zeros((FW, elements), F32)
    for o in range(SECTORS):
        column = jnp.zeros((FW, 128), F32)
        for k in range(NV):
            gain = law_ref[0, o : o + 1, 1 + k : 2 + k] * law_ref[0, o : o + 1, 0:1]
            column = jnp.where(v == k, gain, column)
        column = jnp.concatenate([column] * (elements // 128), axis=1)
        weight = jnp.where(owned_ref[o : o + 1, :] > 0.5, column, weight)
    gain_ref[...] = weight * squares
    state = prism_ref[...]
    prism_part_ref[...] = state.astype(F32) - STEP * mm(prism_volume_ref[...], square_half(state))
    state = tet_ref[...]
    tet_part_ref[...] = state.astype(F32) - STEP * mm(volume_ref[...], square_half(state))
    pad_ref[...] = mm(lift_ref[...], spread(4 * FP, 4 * FW), NT).astype(BF)
    capacity = live_ref.shape[1] // 2
    slot = cols_of((1, capacity))
    for side in range(2):
        area = area_ref[:, side * capacity : (side + 1) * capacity]
        live_ref[:, side * capacity : (side + 1) * capacity] = jnp.where(slot < count_ref[:, side : side + 1], area, 0.0)


def wall_kernel(
    burn_hbm, owner_hbm, prism_hbm, wall_hbm, tet_hbm, code_hbm, extrap_hbm,
    volume_hbm, prism_volume_hbm, lift_hbm, law_hbm, count_hbm, area_hbm,
    part_ref, owned_ref, prism_ref, wall_ref, tet_ref, code_ref, extrap_ref,
    odd_ref, even_ref, tet_part_ref, prism_part_ref, rows_ref, gain_ref, pad_ref, live_ref,
    burn_ref, owner_ref, volume_ref, prism_volume_ref, lift_ref, law_ref, count_ref, area_ref, sems,
):
    pairs = (
        (burn_hbm, burn_ref), (owner_hbm, owner_ref), (prism_hbm, prism_ref), (wall_hbm, wall_ref),
        (tet_hbm, tet_ref), (code_hbm, code_ref), (extrap_hbm, extrap_ref),
    )
    copies = [pltpu.make_async_copy(a, b, sems.at[n]) for n, (a, b) in enumerate(pairs)]
    for copy in copies:
        copy.start()
    for copy in copies[:2]:
        copy.wait()
    walls = burn_ref.shape[1]
    place = hot(rows_of((prism_ref.shape[1], walls)) == burn_ref[...])
    owned = mm(hot(rows_of((8, walls)) == owner_ref[...]), place, NT)
    owned_ref[...] = owned
    for copy in copies[2:4]:
        copy.wait()
    rows = mm(wall_ref[(NV - 1) * TFP : NV * TFP, :], prism_ref[...]).astype(BF).astype(F32)
    sums = jnp.sum(rows * rows, axis=0, keepdims=True)
    part_ref[...] = jnp.broadcast_to(jnp.sum(owned * sums, axis=1, keepdims=True), part_ref.shape)
    for copy in copies[4:]:
        copy.wait()

    @pl.when(early())
    def _():
        more = (
            (volume_hbm, volume_ref), (prism_volume_hbm, prism_volume_ref), (lift_hbm, lift_ref),
            (law_hbm, law_ref), (count_hbm, count_ref), (area_hbm, area_ref),
        )
        late = [pltpu.make_async_copy(a, b, sems.at[len(pairs) + n]) for n, (a, b) in enumerate(more)]
        for copy in late:
            copy.start()
        make_faces(code_ref, tet_ref, extrap_ref, odd_ref, even_ref)
        for copy in late:
            copy.wait()
        make_local(
            tet_ref, prism_ref, wall_ref, owned_ref, volume_ref, prism_volume_ref, lift_ref, law_ref, count_ref, area_ref,
            tet_part_ref, prism_part_ref, rows_ref, gain_ref, pad_ref, live_ref,
        )


def face_kernel(code_ref, tet_ref, extrap_ref, odd_in, even_in, odd_ref, even_ref):
    axial = lax.axis_index("axial")

    @pl.when(jnp.logical_not(early()) & (axial > 0))
    def _():
        make_faces(code_ref, tet_ref, extrap_ref, odd_ref, even_ref)

    @pl.when(jnp.logical_not(early()) & (axial == 0))
    def _():
        capacity = odd_ref.shape[1]
        pad = mm(spread(4 * FP, 4 * FW), extrap_ref[...], NT).astype(BF)
        odd_ref[...] = jnp.zeros_like(odd_ref)
        even_ref[...] = faces_of(code_ref[:, capacity:], tet_ref[...], pad)


def local_kernel(
    tet_ref, prism_ref, wall_ref, owned_ref, volume_ref, prism_volume_ref, lift_ref, law_ref, count_ref, area_ref,
    tet_part_in, prism_part_in, rows_in, gain_in, pad_in, live_in,
    tet_part_ref, prism_part_ref, rows_ref, gain_ref, pad_ref, live_ref,
):
    @pl.when(jnp.logical_not(early()))
    def _():
        make_local(
            tet_ref, prism_ref, wall_ref, owned_ref, volume_ref, prism_volume_ref, lift_ref, law_ref, count_ref, area_ref,
            tet_part_ref, prism_part_ref, rows_ref, gain_ref, pad_ref, live_ref,
        )


def tet_kernel(code_ref, live_ref, odd_ref, even_ref, from_odd_ref, from_even_ref, part_ref, pad_ref, out_ref):
    first = first_side()
    capacity = even_ref.shape[1]
    elements = part_ref.shape[1]
    placed = None
    for side, own, other in ((1 - first, odd_ref, from_odd_ref), (first, even_ref, from_even_ref)):
        code = side_of(code_ref, side)
        live = side_of(live_ref, side)
        normal = jnp.where(side == 0, -0.25, 0.25)
        left = own[...].astype(F32)
        right = other[...].astype(F32)
        speed = jnp.maximum(jnp.abs(left), jnp.abs(right))
        flux = normal * (right * right - left * left) - 0.5 * speed * (right - left)
        jump = (live * flux).astype(BF)
        face = code & 3
        masked = jnp.concatenate([jnp.where(face == f, jump, jnp.zeros_like(jump)) for f in range(4)], axis=0)
        pick = hot(rows_of((elements, capacity)) == (code >> 2))
        piece = mm(masked, pick, NT)
        placed = piece if placed is None else placed + piece
    out_ref[...] = (part_ref[...] - STEP * mm(pad_ref[...], placed.astype(BF))).astype(BF)


def prism_kernel(
    tet_ref, pair_ref, other_ref, law_ref, owned_ref, rows_ref, gain_ref, part_ref, lift_ref,
    tet_hbm, prism_hbm, prism_ref, sems,
):
    tet_out = pltpu.make_async_copy(tet_ref, tet_hbm, sems.at[0])
    tet_out.start()
    sums = (pair_ref[...] + other_ref[...])[:SECTORS]
    damping = 1.0 / (1.0 + law_ref[0, :, 0:1] * sums / (BW_DEV * TFP))
    elements = part_ref.shape[1]
    width = elements // 8
    lift = lift_ref[...]
    outs = []
    for n in range(8):
        at = slice(n * width, (n + 1) * width)
        factor = jnp.zeros((1, width), F32)
        for o in range(SECTORS):
            row = jnp.concatenate([damping[o : o + 1]] * (width // 128), axis=1)
            factor = jnp.where(owned_ref[o : o + 1, at] > 0.5, row, factor)
        jump = (gain_ref[:, at] * factor - rows_ref[:, at]).astype(BF)
        prism_ref[:, at] = (part_ref[:, at] - STEP * mm(lift, jump, TN)).astype(BF)
        out = pltpu.make_async_copy(prism_ref.at[:, at], prism_hbm.at[:, at], sems.at[1 + n])
        out.start()
        outs.append(out)
    for out in outs:
        out.wait()
    tet_out.wait()


VM = pl.BlockSpec(memory_space=pltpu.VMEM)
HB = pl.BlockSpec(memory_space=pltpu.HBM)


def call(kernel, name, outs, out_specs, specs, flops, moved, args, scratch=(), aliases=()):
    return pl.pallas_call(
        kernel,
        out_shape=outs,
        in_specs=specs,
        out_specs=out_specs,
        scratch_shapes=scratch,
        input_output_aliases=dict(aliases),
        cost_estimate=pl.CostEstimate(flops=flops, bytes_accessed=moved, transcendentals=0),
        compiler_params=pltpu.CompilerParams(vmem_limit_bytes=32 * 1024 * 1024),
        name=name,
    )(*args)


def like(value):
    return pltpu.VMEM(value.shape, value.dtype)


def swap(value, axis, pairs):
    return lax.ppermute(value, axis, list(pairs) + [(j, i) for i, j in pairs])


def on_device(
    tet_state,
    prism_state,
    tet_volume,
    prism_volume,
    face_extrap,
    face_lift,
    wall_extrap,
    wall_lift,
    face_code,
    face_count,
    face_area,
    burn_prism,
    burn_owner,
    burn_law,
):
    slots = face_code.shape[0]
    capacity = slots // 2
    code = face_code.reshape(1, slots)
    area = face_area.reshape(1, slots)
    burn = burn_prism.reshape(1, -1)
    owner = burn_owner.reshape(1, -1)
    extrap = face_extrap.T
    wall_lift = wall_lift.T
    tall = prism_state.shape[1]
    side = pltpu.VMEM((FP, capacity), BF)
    hbm = pltpu.with_memory_space_constraint
    operands = (burn, owner, prism_state, wall_extrap, tet_state, code, extrap)
    more = (tet_volume, prism_volume, face_lift, burn_law, face_count, area)
    local_outs = (
        pltpu.VMEM(tet_state.shape, F32),
        pltpu.VMEM(prism_state.shape, F32),
        pltpu.VMEM((FW, tall), F32),
        pltpu.VMEM((FW, tall), F32),
        pltpu.VMEM((tet_state.shape[0], 4 * FP), BF),
        like(area),
    )
    part, owned, prism, wall, tet, code, extrap, odd, even, *made = call(
        wall_kernel,
        "walls",
        (pltpu.VMEM((8, 128), F32), pltpu.VMEM((8, tall), F32))
        + tuple(like(x) for x in operands[2:])
        + (side, side)
        + local_outs,
        (VM,) * 15,
        [HB] * 13,
        5_000_000_000,
        3_000_000,
        tuple(hbm(x, pltpu.HBM) for x in operands + more),
        [like(x) for x in operands[:2] + more] + [pltpu.SemaphoreType.DMA((13,))],
    )
    odd, even = call(
        face_kernel, "faces", (side, side), (VM, VM), [VM] * 5, 5_000_000_000, 600_000, (code, tet, extrap, odd, even),
        aliases=((3, 0), (4, 1)),
    )
    part, tet_volume, prism_volume, face_lift, wall_lift, law, face_count, area = lax.optimization_barrier(
        (part, tet_volume, prism_volume, face_lift, wall_lift, burn_law, face_count, area)
    )
    half = swap(part, "azim", ((0, 3), (1, 2)))
    count = lax.axis_size("axial")
    from_even = swap(even, "axial", [(i, i + 1) for i in range(0, count - 1, 2)])
    from_odd = swap(odd, "axial", [(i, i + 1) for i in range(1, count - 1, 2)])
    pair = part + half
    other = swap(pair, "azim", ((0, 1), (2, 3)))
    pair, tet, prism = lax.optimization_barrier((pair, tet, prism))
    tet_part, prism_part, rows, gain, pad, live = call(
        local_kernel,
        "local",
        local_outs,
        (VM,) * 6,
        [VM] * 16,
        5_000_000_000,
        4_000_000,
        (tet, prism, wall, owned, tet_volume, prism_volume, face_lift, law, face_count, area, *made),
        aliases=tuple((10 + n, n) for n in range(6)),
    )
    tet_new = call(
        tet_kernel,
        "tet_finish",
        like(tet),
        VM,
        [VM] * 8,
        5_000_000_000,
        3_000_000,
        (code, live, odd, even, from_odd, from_even, tet_part, pad),
    )
    tet_new, prism_new = call(
        prism_kernel,
        "prism_finish",
        (jax.ShapeDtypeStruct(tet.shape, BF), jax.ShapeDtypeStruct(prism.shape, BF)),
        (HB, HB),
        [VM] * 9,
        5_000_000_000,
        3_000_000,
        (tet_new, pair, other, law, owned, rows, gain, prism_part, wall_lift),
        [like(prism), pltpu.SemaphoreType.DMA((9,))],
    )
    return (tet_new, prism_new)


def solution(mesh):
    elements = P(None, ("axial", "azim"))
    placed = (
        elements,
        elements,
        P(),
        P(),
        P(),
        P(),
        P(),
        P(),
        P(("axial", "azim")),
        P(("axial", "azim"), None),
        P(("axial", "azim")),
        P(("axial", "azim")),
        P(("axial", "azim"), None),
        P("axial", None, None),
    )
    return jax.shard_map(
        on_device, mesh=mesh, in_specs=placed, out_specs=(elements, elements), check_vma=False
    )
```
